32 devices in a mesh: groups: 2 (over y), ctx: 4 (over z), head: 4 (over x, core).
Axes of the slice: x: 2, y: 2, z: 4, core: 2. Of those that a mesh axis runs over, the one named last changes fastest.
Arguments:
- queries: bfloat16 [64, 128, 576], P(('groups', 'ctx'), 'head'), parts along dimension 0, may hold values from -1024 to 1024
- out_grad: bfloat16 [64, 128, 512], P(('groups', 'ctx'), 'head'), parts along dimension 0, may hold values from -6 to 6
- latents: bfloat16 [32, 1024, 576], P(None, ('groups', 'ctx', 'head')), parts along dimension 1, may hold values from -16 to 16
- index_keys: bfloat16 [32, 1024, 128], P(None, ('groups', 'ctx', 'head')), parts along dimension 1, may hold values from -16 to 16
- index_queries: bfloat16 [64, 64, 128], P(('groups', 'ctx'), 'head'), parts along dimension 0, may hold values from -256 to 256
- index_weights: float32 [64, 64], P(('groups', 'ctx'), 'head'), parts along dimension 0, may hold values from -1 to 1
- picked_blocks: int32 [64, 4], P(('groups', 'ctx')), parts along dimension 0, may hold values from -1 to 127, as said below
- key_reach: int32 [32768], P('groups'), parts along dimension 0, may hold values from 1 to 16384, as said below
Outputs:
- query_grad: bfloat16 [64, 128, 576], P(('groups', 'ctx'), 'head'), parts along dimension 0
- latent_grad: float32 [32, 1024, 576], P(None, ('groups', 'ctx', 'head')), parts along dimension 1
- index_query_grad: bfloat16 [64, 64, 128], P(('groups', 'ctx'), 'head'), parts along dimension 0
- index_weight_grad: float32 [64, 64], P(('groups', 'ctx'), 'head'), parts along dimension 0
- index_key_grad: float32 [32, 1024, 128], P(None, ('groups', 'ctx', 'head')), parts along dimension 1
The draws below stay inside these ranges and needn't reach their ends.
There are 2 independent parts, one for each index of `groups`. The reference program is written for one: setup_inputs(seed, part) draws one part's arguments, and reference() takes and returns one part's arrays. A program takes and returns all parts, laid end to end along the dimension named above; each array names one. Nothing has to cross between parts.
Inputs may be any that keep to these rules, and one draw needn't show every extreme that they name: `picked_blocks`: each row lists distinct key blocks (block b covers positions b * 128 to b * 128 + 127): first the block of the row's own query position, then blocks that lie wholly before it; -1 marks unused entries, which come only after all used ones. Among the rows of one device (aligned blocks of 8 rows) no two different blocks leave the same remainder modulo 128 // 32. key_reach[p] is the end (exclusive) of the subtree of the tree node that holds position p, nodes packed in depth-first order: p < key_reach[p], and the ranges from p to key_reach[p] of any two positions are nested or disjoint.
All inputs are finite; a program needn't handle non-finite values.
Results may differ from the reference program's by a relative error of at most 0.0049.
Values may be sent and summed in bfloat16 or wider, within the bound.
A program may use at most 256 MiB of HBM per device.

```python
import jax
import jax.numpy as jnp
from jax import lax

HEADS = 128
LAT = 512
ROPE = 64
IHEADS = 64
IDIM = 128
QK_DIM = 192
BLOCK = 128
Q_DEV = 8
OWN_BLOCKS = 32
PICKS = 4
BLOCKS = 128
CONTEXT = 16384
BAND = 32
N_CTX = 4


def latent_draw(key):
    key = jax.random.fold_in(key, 201)
    first_key = jax.random.fold_in(key, 0)
    values = jnp.clip(jax.random.normal(first_key, (CONTEXT, LAT + ROPE), jnp.float32), -6.0, 6.0)
    return values.astype(jnp.bfloat16).astype(jnp.float32)


def index_key_draw(key):
    key = jax.random.fold_in(key, 202)
    first_key = jax.random.fold_in(key, 0)
    values = jnp.clip(jax.random.normal(first_key, (CONTEXT, IDIM), jnp.float32), -6.0, 6.0)
    return values.astype(jnp.bfloat16).astype(jnp.float32)


def weight_draw(key):
    key = jax.random.fold_in(key, 203)
    first_key = jax.random.fold_in(key, 0)
    normal_part = jnp.clip(0.125 * jax.random.normal(first_key, (BAND, IHEADS), jnp.float32), -0.75, 0.75)
    return normal_part


def tree_draw(key):
    key = jax.random.fold_in(key, 204)
    first_key, second_key = jax.random.split(key)
    positions = jnp.arange(CONTEXT, dtype=jnp.int32)
    starts = (jax.random.randint(first_key, (CONTEXT,), 0, 3 * BLOCK) == 0) & (positions >= CONTEXT // 8)
    starts = starts | (positions == 0)
    depths = jnp.where(positions == 0, 0, jax.random.randint(second_key, (CONTEXT,), 1, 9)).astype(jnp.int32)
    seg_begin = lax.cummax(jnp.where(starts, positions, 0), axis=0)
    levels = depths[seg_begin]
    end_table = []
    for bound_level in range(9):
        candidate = jnp.where(starts & (depths <= bound_level), positions, CONTEXT).astype(jnp.int32)
        following = jnp.concatenate([candidate[1:], jnp.full((1,), CONTEXT, jnp.int32)])
        end_table.append(lax.cummin(following, axis=0, reverse=True))
    reaches = jnp.take_along_axis(jnp.stack(end_table), levels[None, :], axis=0)[0]
    return reaches.astype(jnp.int32)


def draw_queries(key, part):
    key = jax.random.fold_in(key, 11)
    first_key = jax.random.fold_in(key, 0)
    queries_out = jnp.clip(jax.random.normal(first_key, (BAND, HEADS, LAT + ROPE), jnp.float32), -6.0, 6.0)
    return queries_out.astype(jnp.bfloat16)


def draw_latents(key, part):
    return latent_draw(key).reshape(OWN_BLOCKS, N_CTX * BLOCK, LAT + ROPE).astype(jnp.bfloat16)


def draw_index_keys(key, part):
    return index_key_draw(key).reshape(OWN_BLOCKS, N_CTX * BLOCK, IDIM).astype(jnp.bfloat16)


def draw_index_weights(key, part):
    return weight_draw(key)


def draw_index_queries(key, part):
    key = jax.random.fold_in(key, 13)
    iqueries = jnp.clip(jax.random.normal(key, (BAND, IHEADS, IDIM), jnp.float32), -6.0, 6.0) * IDIM ** (-0.5)
    return iqueries.astype(jnp.bfloat16)


def draw_key_reach(key, part):
    reaches = tree_draw(key)
    return reaches


def draw_picked_blocks(key, part):
    reaches = tree_draw(key)
    key = jax.random.fold_in(key, 17)
    first_key, second_key, third_key = jax.random.split(key, 3)
    positions = jnp.arange(CONTEXT, dtype=jnp.int32)
    devices = jnp.arange(N_CTX, dtype=jnp.int32)
    first_place = CONTEXT - BAND + devices * Q_DEV
    home_block = first_place // BLOCK
    seen_rows = (positions[None, :] <= first_place[:, None]) & (reaches[None, :] > first_place[:, None])
    seen_block = jnp.any(seen_rows.reshape(N_CTX, BLOCKS, BLOCK), axis=-1)
    block_ids = jnp.arange(BLOCKS, dtype=jnp.int32)
    allowed = (seen_block & (block_ids[None, :] < home_block[:, None])).reshape(N_CTX, OWN_BLOCKS, N_CTX)
    ranking = jax.random.randint(first_key, (N_CTX, N_CTX, OWN_BLOCKS), 1, 1 << 20) * OWN_BLOCKS + jnp.arange(OWN_BLOCKS, dtype=jnp.int32)
    ranking = jnp.where(jnp.swapaxes(allowed, 1, 2), ranking, 0)
    top_rank, top_round = lax.top_k(ranking, 1)
    home_owner = home_block % N_CTX
    present = (top_rank[:, :, 0] > 0) & (devices[None, :] != home_owner[:, None])
    candidates = top_round[:, :, 0] * N_CTX + devices[None, :]
    row_device = jnp.arange(BAND, dtype=jnp.int32) // Q_DEV
    row_rank = jax.random.randint(second_key, (BAND, N_CTX), 1, 1 << 20) * N_CTX + devices[None, :]
    row_rank = jnp.where(present[row_device], row_rank, 0)
    pick_rank, pick_owner = lax.top_k(row_rank, PICKS - 1)
    others = jnp.take_along_axis(candidates[row_device], pick_owner, axis=1)
    extra_count = jnp.minimum(jax.random.randint(third_key, (BAND, 1), 0, 2 * PICKS), PICKS - 1)
    kept_mask = (pick_rank > 0) & (jnp.arange(PICKS - 1, dtype=jnp.int32)[None, :] < extra_count)
    others = jnp.where(kept_mask, others, -1)
    return jnp.concatenate([home_block[row_device][:, None], others], axis=1).astype(jnp.int32)


def level_of(rng, extent, cuts, smallest, largest):
    level, own = 1.0, jax.random.fold_in(rng, 6)
    for position, blocks in cuts:
        heights = jnp.exp(jax.random.uniform(jax.random.fold_in(own, position), (blocks,), jnp.float32, smallest / len(cuts), largest / len(cuts)))
        level = level * jnp.repeat(heights, extent[position] // blocks).reshape([-1 if axis == position else 1 for axis in range(len(extent))])
    return level


def noise(key, shape, scale, most, pieces=(), held_as=jnp.bfloat16):
    result = jax.random.normal(key, shape, jnp.float32) * scale
    if len(pieces) > 0:
        result = level_of(key, shape, pieces, -0.22, 0.18) * result
    return jnp.clip(result, min=-most, max=most).astype(held_as)


def setup_inputs(seed: int = 0, part: int = 0) -> dict:
    key_list = jax.random.split(jax.random.key(seed), 9)
    own_keys = jax.random.split(jax.random.fold_in(key_list[8], part), 9)
    return {
        "queries": draw_queries(jax.random.fold_in(jax.random.fold_in(key_list[8], part), 71), part),
        "out_grad": noise(own_keys[1], (BAND, HEADS, LAT), 1.0, 6.0, ((0, 4), (1, 4))),
        "latents": draw_latents(jax.random.fold_in(jax.random.fold_in(key_list[8], part), 71), part),
        "index_keys": draw_index_keys(jax.random.fold_in(jax.random.fold_in(key_list[8], part), 71), part),
        "index_queries": draw_index_queries(jax.random.fold_in(jax.random.fold_in(key_list[8], part), 71), part),
        "index_weights": draw_index_weights(jax.random.fold_in(jax.random.fold_in(key_list[8], part), 71), part),
        "picked_blocks": draw_picked_blocks(jax.random.fold_in(jax.random.fold_in(key_list[8], part), 71), part),
        "key_reach": draw_key_reach(jax.random.fold_in(jax.random.fold_in(key_list[8], part), 71), part),
    }


SCORE_FLOOR = -1.0e30


def masked_softmax(scores, visible):
    highest = jnp.max(jnp.where(visible, scores, SCORE_FLOOR), axis=-1, keepdims=True)
    weights = jnp.where(visible, jnp.exp(jnp.where(visible, scores - highest, 0.0)), 0.0)
    return weights / jnp.sum(weights, axis=-1, keepdims=True)


def bf16_round(values):
    narrow = lax.optimization_barrier(values.astype(jnp.bfloat16))
    return narrow.astype(jnp.float32)


def reference(queries, out_grad, latents, index_keys, index_queries, index_weights, picked_blocks, key_reach):
    key_width = LAT + ROPE
    score_scale = QK_DIM ** -0.5
    latent_flat = latents.reshape(CONTEXT, key_width)
    index_flat = index_keys.reshape(CONTEXT, IDIM)
    groups = BAND // Q_DEV
    positions = (CONTEXT - BAND + jnp.arange(BAND, dtype=jnp.int32)).astype(jnp.int32)
    offsets = jnp.arange(BLOCK, dtype=jnp.int32)

    def group_step(carried, inputs):
        latent_acc, index_acc = carried
        query_rows, grad_rows, iquery_rows, weight_rows, pick_rows, place_rows = inputs
        usable = pick_rows >= 0
        key_pos = (jnp.where(usable, pick_rows, 0)[:, :, None] * BLOCK + offsets[None, None, :])
        key_pos = key_pos.reshape(Q_DEV, PICKS * BLOCK).astype(jnp.int32)
        visible = jnp.repeat(usable, BLOCK, axis=1) & (key_pos <= place_rows[:, None]) & (place_rows[:, None] < key_reach[key_pos])
        gathered = latent_flat[key_pos].astype(jnp.float32)
        gathered_index = index_flat[key_pos].astype(jnp.float32)
        query_wide = query_rows.astype(jnp.float32)
        grad_wide = grad_rows.astype(jnp.float32)
        index_wide = iquery_rows.astype(jnp.float32)
        scores = jnp.einsum("qhd,qkd->qhk", query_wide, gathered) * score_scale
        attention = masked_softmax(scores, visible[:, None, :])
        value_pull = jnp.einsum("qhd,qkd->qhk", grad_wide, gathered[:, :, :LAT])
        row_inner = jnp.sum(attention * value_pull, axis=-1, keepdims=True)
        score_grad = bf16_round(score_scale * attention * (value_pull - row_inner))
        attention_low = bf16_round(attention)
        query_grad = jnp.einsum("qhk,qkd->qhd", score_grad, gathered).astype(jnp.bfloat16)
        key_grad = jnp.einsum("qhk,qhd->qkd", score_grad, query_wide)
        value_grad = jnp.einsum("qhk,qhd->qkd", attention_low, grad_wide)
        key_grad = key_grad + jnp.pad(value_grad, ((0, 0), (0, 0), (0, ROPE)))
        latent_acc = latent_acc.at[key_pos.reshape(-1)].add(key_grad.reshape(-1, key_width))
        target = jnp.sum(attention, axis=1) / HEADS
        index_score = jnp.einsum("qgd,qkd->qgk", index_wide, gathered_index)
        positive = jnp.maximum(index_score, 0.0)
        logits = jnp.sum(weight_rows[:, :, None] * positive, axis=1)
        index_probs = masked_softmax(logits, visible)
        logit_grad = index_probs - target
        weight_grad = jnp.sum(logit_grad[:, None, :] * positive, axis=-1)
        spread = bf16_round(jnp.where(index_score > 0.0, logit_grad[:, None, :] * weight_rows[:, :, None], 0.0))
        iquery_grad = jnp.einsum("qgk,qkd->qgd", spread, gathered_index).astype(jnp.bfloat16)
        ikey_grad = jnp.einsum("qgk,qgd->qkd", spread, index_wide)
        index_acc = index_acc.at[key_pos.reshape(-1)].add(ikey_grad.reshape(-1, IDIM))
        return (latent_acc, index_acc), (query_grad, iquery_grad, weight_grad)

    start_state = (jnp.zeros((CONTEXT, key_width), jnp.float32), jnp.zeros((CONTEXT, IDIM), jnp.float32))
    sliced = (queries.reshape(groups, Q_DEV, HEADS, key_width),
              out_grad.reshape(groups, Q_DEV, HEADS, LAT),
              index_queries.reshape(groups, Q_DEV, IHEADS, IDIM),
              index_weights.reshape(groups, Q_DEV, IHEADS),
              picked_blocks.reshape(groups, Q_DEV, PICKS),
              positions.reshape(groups, Q_DEV))
    finals, stacked = lax.scan(group_step, start_state, sliced)
    latent_acc, index_acc = finals
    query_all, iquery_all, weight_all = stacked
    return (query_all.reshape(BAND, HEADS, key_width),
            latent_acc.reshape(OWN_BLOCKS, N_CTX * BLOCK, key_width),
            iquery_all.reshape(BAND, IHEADS, IDIM),
            weight_all.reshape(BAND, IHEADS),
            index_acc.reshape(OWN_BLOCKS, N_CTX * BLOCK, IDIM))
```

```python
import functools

import jax
import jax.numpy as jnp
from jax import lax
from jax.experimental import pallas as pl
from jax.experimental.pallas import tpu as pltpu
from jax.sharding import PartitionSpec as P

HEADS = 128
QK_DIM = 192
SCORE_FLOOR = -1e30
LANES = 128
MESH = pl.DeviceIdType.MESH
VMEM_BYTES = 56 * 1024 * 1024

NT = (((1,), (1,)), ((), ()))
TN = (((0,), (0,)), ((), ()))
NN = (((1,), (0,)), ((), ()))


def dot(a, b, dims):
    return lax.dot_general(a, b, dims, preferred_element_type=jnp.float32)


def exchange_kernel(
    owners,
    heads,
    sizes,
    q_hbm,
    g_hbm,
    lat_hbm,
    key_hbm,
    iq_ref,
    iw_ref,
    pick_ref,
    reach_hbm,
    qg_ref,
    back_lat_ref,
    back_key_ref,
    iqg_ref,
    iwg_ref,
    home_ref,
    q_buf,
    g_buf,
    lat_buf,
    key_buf,
    reach_buf,
    want_buf,
    asked,
    row_send,
    rows,
    part,
    glat,
    gkey,
    rlat,
    rkey,
    hlat,
    hkey,
    local_sem,
    ask_s,
    ask_r,
    row_s,
    row_r,
    fwd_s,
    fwd_r,
    part_s,
    part_r,
    glat_s,
    glat_r,
    gkey_s,
    gkey_r,
    hlat_s,
    hlat_r,
    hkey_s,
    hkey_r,
):
    row_count, local_heads, key_width, latent_width, shard_rows, context = sizes
    key_at = -(-key_width // LANES) * LANES
    block_rows = shard_rows * heads
    shift = owners.bit_length() - 1
    me_c = lax.axis_index("ctx")
    me_h = lax.axis_index("head")

    def ctx_at(step):
        return lax.rem(me_c + step + owners, owners)

    def head_at(step):
        return lax.rem(me_h + step + heads, heads)

    def remote(src, dst, send_sem, recv_sem, **where):
        return pltpu.make_async_remote_copy(
            src_ref=src,
            dst_ref=dst,
            send_sem=send_sem,
            recv_sem=recv_sem,
            device_id=where,
            device_id_type=MESH,
        )

    loads = [
        pltpu.make_async_copy(src, dst, local_sem.at[number])
        for number, (src, dst) in enumerate(
            (
                (lat_hbm, lat_buf),
                (key_hbm, key_buf),
                (reach_hbm, reach_buf),
                (q_hbm, q_buf),
                (g_hbm, g_buf),
            )
        )
    ]
    for load in loads:
        load.start()
    barrier = pltpu.get_barrier_semaphore()
    for step in range(1, owners):
        pl.semaphore_signal(
            barrier, inc=1, device_id={"ctx": ctx_at(step)}, device_id_type=MESH
        )
    for step in range(1, heads):
        pl.semaphore_signal(
            barrier, inc=1, device_id={"head": head_at(step)}, device_id_type=MESH
        )

    lane = lax.broadcasted_iota(jnp.int32, (row_count, LANES), 1)
    picked = pick_ref[...]
    by_row = jnp.full((row_count, LANES), -1, jnp.int32)
    for number in range(picked.shape[1]):
        column = jnp.broadcast_to(picked[:, number : number + 1], (row_count, LANES))
        match = (column >= 0) & ((column & (owners - 1)) == lane)
        by_row = jnp.where(match, column >> shift, by_row)
    wanted = jnp.max(by_row, axis=0, keepdims=True)
    want_buf[...] = jnp.broadcast_to(wanted, want_buf.shape)
    pl.semaphore_wait(barrier, owners + heads - 2)

    asks = []
    for step in range(1, owners):
        copy = remote(
            want_buf,
            asked.at[step - 1],
            ask_s.at[step - 1],
            ask_r.at[step - 1],
            ctx=ctx_at(step),
        )
        copy.start()
        asks.append(copy)

    def forward(step):
        copies = []
        for turn in range(1, heads):
            slot = rows.at[ctx_at(-step), me_h]
            copy = remote(
                slot, slot, fwd_s.at[step, turn - 1], fwd_r.at[step, turn - 1], head=head_at(turn)
            )
            copy.start()
            copies.append(copy)
        return copies

    loads[0].wait()
    loads[1].wait()
    first_lane = lax.broadcasted_iota(jnp.int32, (1, LANES), 1)
    own_round = jnp.max(jnp.where(first_lane == me_c, wanted, -1))
    at = jnp.maximum(own_round, 0)
    rows[me_c, me_h, :, :key_width] = lat_buf[at]
    rows[me_c, me_h, :, key_at:] = key_buf[at]
    homes = [own_round]
    sends = list(forward(0))
    row_copies = []
    for step in range(1, owners):
        asks[step - 1].wait_recv()
        told = jnp.max(jnp.where(first_lane == me_c, asked[step - 1, 0:1, :], -1))
        homes.append(told)
        at = jnp.maximum(told, 0)
        row_send[step - 1, :, :key_width] = lat_buf[at]
        row_send[step - 1, :, key_at:] = key_buf[at]
        copy = remote(
            row_send.at[step - 1],
            rows.at[me_c, me_h],
            row_s.at[owners - step - 1],
            row_r.at[owners - step - 1],
            ctx=ctx_at(-step),
        )
        copy.start()
        row_copies.append(copy)
    home_lane = lax.broadcasted_iota(jnp.int32, home_ref.shape, 1)
    home_all = jnp.full(home_ref.shape, -1, jnp.int32)
    for step in range(owners):
        home_all = jnp.where(home_lane == step, homes[step], home_all)
    home_ref[...] = home_all

    loads[2].wait()
    first_pos = context - row_count * owners + me_c * row_count
    places = first_pos + lax.broadcasted_iota(jnp.int32, (row_count, block_rows), 0)
    offsets = lax.broadcasted_iota(jnp.int32, (row_count, block_rows), 1)
    seen = []
    for owner in range(owners):
        block = (
            jnp.maximum(jnp.max(jnp.where(first_lane == owner, wanted, -1)), 0) * owners + owner
        )
        ends = jnp.broadcast_to(reach_buf[pl.ds(block, 1), :], places.shape)
        used = jnp.broadcast_to(by_row[:, owner : owner + 1], places.shape) >= 0
        ok = used & (block * block_rows + offsets <= places) & (places < ends)
        seen.append(jnp.where(ok, 1.0, 0.0))
    visible = jnp.concatenate(seen, axis=1)
    key_count = owners * block_rows

    for step in range(1, owners):
        slot = rows.at[ctx_at(-step), me_h]
        remote(
            row_send.at[0], slot, row_s.at[step - 1], row_r.at[step - 1], ctx=ctx_at(step)
        ).wait_recv()
        sends += forward(step)
    for step in range(owners):
        for turn in range(1, heads):
            slot = rows.at[ctx_at(-step), head_at(-turn)]
            remote(
                slot, slot, fwd_s.at[step, turn - 1], fwd_r.at[step, turn - 1], head=head_at(turn)
            ).wait_recv()

    loads[3].wait()
    loads[4].wait()
    stack = row_count * local_heads
    keys = rows[:, :, :, :key_width].reshape(key_count, key_width)
    ikeys = rows[:, :, :, key_at:].reshape(key_count, rows.shape[3] - key_at)
    queries = q_buf[...].reshape(stack, key_width)
    grads = g_buf[...].reshape(stack, latent_width)
    index_heads, index_width = iq_ref.shape[1], iq_ref.shape[2]
    index_stack = row_count * index_heads
    iqueries = iq_ref[...].reshape(index_stack, index_width)
    eye = jnp.where(
        lax.broadcasted_iota(jnp.int32, (index_heads, index_heads), 0)
        == lax.broadcasted_iota(jnp.int32, (index_heads, index_heads), 1),
        1.0,
        0.0,
    )
    weights = jnp.sum(iw_ref[...][:, None, :] * eye[None], axis=2, keepdims=True)

    def softmax(scores, mask):
        held = jnp.where(mask, scores, SCORE_FLOOR)
        raised = jnp.exp(held - jnp.max(held, axis=-1, keepdims=True))
        return raised * (1.0 / jnp.sum(raised, axis=-1, keepdims=True))

    score_scale = QK_DIM ** (-0.5)
    index_score = dot(iqueries, ikeys, NT).reshape(row_count, index_heads, key_count)
    positive = jnp.maximum(index_score, 0.0)
    part[me_h, 1] = jnp.sum(weights * positive, axis=1)
    scores = dot(queries, keys, NT).reshape(row_count, local_heads, key_count) * score_scale
    attention = softmax(scores, visible[:, None, :] > 0.5)
    part[me_h, 0] = jnp.sum(attention, axis=1)
    for turn in range(1, heads):
        slot = part.at[me_h]
        copy = remote(slot, slot, part_s.at[turn - 1], part_r.at[turn - 1], head=head_at(turn))
        copy.start()
        sends.append(copy)

    pulls = dot(grads, keys[:, :latent_width], NT).reshape(row_count, local_heads, key_count)
    inner = jnp.sum(attention * pulls, axis=-1, keepdims=True)
    score_grad = (score_scale * attention * (pulls - inner)).astype(jnp.bfloat16)
    score_grad = score_grad.reshape(stack, key_count)
    low = attention.astype(jnp.bfloat16).reshape(stack, key_count)
    key_grad = dot(score_grad, queries, TN)
    value_grad = dot(low, grads, TN)
    parts4 = (owners, heads, shard_rows)
    first = (key_grad[:, :latent_width] + value_grad).astype(jnp.bfloat16)
    first = first.reshape(*parts4, latent_width)
    second = key_grad[:, latent_width:].astype(jnp.bfloat16)
    second = second.reshape(*parts4, key_width - latent_width)
    for head in range(heads):
        glat[head, :, :, :latent_width] = first[:, head]
        glat[head, :, :, latent_width:] = second[:, head]
    for turn in range(1, heads):
        copy = remote(
            glat.at[head_at(turn)],
            rlat.at[turn - 1],
            glat_s.at[turn - 1],
            glat_r.at[turn - 1],
            head=head_at(turn),
        )
        copy.start()
        sends.append(copy)
    qg_ref[...] = (
        dot(score_grad, keys, NN).astype(jnp.bfloat16).reshape(row_count, local_heads, key_width)
    )

    for turn in range(1, heads):
        slot = part.at[head_at(-turn)]
        remote(
            slot, slot, part_s.at[turn - 1], part_r.at[turn - 1], head=head_at(turn)
        ).wait_recv()
    mass, logits = part[0, 0], part[0, 1]
    for head in range(1, heads):
        mass, logits = mass + part[head, 0], logits + part[head, 1]
    logit_grad = softmax(logits, visible > 0.5) - mass * (1.0 / HEADS)
    logit_rows = logit_grad[:, None, :]
    weight_grad = jnp.sum(logit_rows * positive, axis=-1, keepdims=True)
    iwg_ref[...] = jnp.sum(weight_grad * eye[None], axis=1)
    spread = jnp.where(index_score > 0.0, logit_rows * weights, 0.0)
    spread = spread.astype(jnp.bfloat16).reshape(index_stack, key_count)
    index_grad = dot(spread, iqueries, TN).astype(jnp.bfloat16).reshape(*parts4, index_width)
    for head in range(heads):
        gkey[head] = index_grad[:, head]
    for turn in range(1, heads):
        copy = remote(
            gkey.at[head_at(turn)],
            rkey.at[turn - 1],
            gkey_s.at[turn - 1],
            gkey_r.at[turn - 1],
            head=head_at(turn),
        )
        copy.start()
        sends.append(copy)
    iqg_ref[...] = (
        dot(spread, ikeys, NN).astype(jnp.bfloat16).reshape(row_count, index_heads, index_width)
    )

    def reduce_home(own, got, out, back_ref, got_s, got_r, out_s, out_r):
        for turn in range(1, heads):
            remote(
                own.at[0],
                got.at[turn - 1],
                got_s.at[turn - 1],
                got_r.at[turn - 1],
                head=head_at(turn),
            ).wait_recv()
        mine = own.at[me_h]
        for step in range(owners):
            total = mine[ctx_at(step)].astype(jnp.float32)
            for turn in range(1, heads):
                total = total + got[turn - 1, ctx_at(step)].astype(jnp.float32)
            if step == 0:
                back_ref[0] = total.astype(jnp.bfloat16)
                continue
            out[step - 1] = total.astype(jnp.bfloat16)
            copy = remote(
                out.at[step - 1],
                back_ref.at[step],
                out_s.at[step - 1],
                out_r.at[step - 1],
                ctx=ctx_at(step),
            )
            copy.start()
            sends.append(copy)

    reduce_home(glat, rlat, hlat, back_lat_ref, glat_s, glat_r, hlat_s, hlat_r)
    reduce_home(gkey, rkey, hkey, back_key_ref, gkey_s, gkey_r, hkey_s, hkey_r)
    for out, back_ref, out_s, out_r in (
        (hlat, back_lat_ref, hlat_s, hlat_r),
        (hkey, back_key_ref, hkey_s, hkey_r),
    ):
        for step in range(1, owners):
            remote(
                out.at[step - 1],
                back_ref.at[step],
                out_s.at[step - 1],
                out_r.at[step - 1],
                ctx=ctx_at(step),
            ).wait_recv()
    for copy in asks + row_copies + sends:
        copy.wait_send()


def place_kernel(owners, home_ref, lat_ref, key_ref, lat_out, key_out):
    lat_out[...] = jnp.zeros_like(lat_out)
    key_out[...] = jnp.zeros_like(key_out)
    for step in range(owners):
        at = jnp.maximum(home_ref[0, step], 0)
        lat_out[at] = lat_out[at] + lat_ref[step].astype(jnp.float32)
        key_out[at] = key_out[at] + key_ref[step].astype(jnp.float32)


def shards(
    queries, out_grad, latents, index_keys, index_queries, index_weights, picked_blocks, key_reach
):
    owners = lax.axis_size("ctx")
    heads = lax.axis_size("head")
    row_count, local_heads, key_width = queries.shape
    latent_width = out_grad.shape[2]
    own_count, shard_rows = latents.shape[:2]
    index_width = index_keys.shape[2]
    context = key_reach.shape[0]
    block_rows = shard_rows * heads
    key_count = owners * block_rows
    wide = -(-key_width // LANES) * LANES + index_width
    sizes = (row_count, local_heads, key_width, latent_width, shard_rows, context)
    low, full, whole = jnp.bfloat16, jnp.float32, jnp.int32
    vmem = pl.BlockSpec(memory_space=pltpu.VMEM)
    anywhere = pl.BlockSpec(memory_space=pl.ANY)
    sem = pltpu.SemaphoreType.DMA
    side, turns = max(owners - 1, 1), max(heads - 1, 1)
    query_grad, back_lat, back_key, iquery_grad, weight_grad, home = pl.pallas_call(
        functools.partial(exchange_kernel, owners, heads, sizes),
        out_shape=(
            jax.ShapeDtypeStruct(queries.shape, low),
            jax.ShapeDtypeStruct((owners, shard_rows, key_width), low),
            jax.ShapeDtypeStruct((owners, shard_rows, index_width), low),
            jax.ShapeDtypeStruct(index_queries.shape, low),
            jax.ShapeDtypeStruct(index_weights.shape, full),
            jax.ShapeDtypeStruct((8, LANES), whole),
        ),
        in_specs=[anywhere, anywhere, anywhere, anywhere, vmem, vmem, vmem, anywhere],
        out_specs=(vmem,) * 6,
        scratch_shapes=[
            pltpu.VMEM(queries.shape, low),
            pltpu.VMEM(out_grad.shape, low),
            pltpu.VMEM(latents.shape, low),
            pltpu.VMEM(index_keys.shape, low),
            pltpu.VMEM((context // block_rows, block_rows), whole),
            pltpu.VMEM((8, LANES), whole),
            pltpu.VMEM((side, 8, LANES), whole),
            pltpu.VMEM((side, shard_rows, wide), low),
            pltpu.VMEM((owners, heads, shard_rows, wide), low),
            pltpu.VMEM((heads, 2, row_count, key_count), full),
            pltpu.VMEM((heads, owners, shard_rows, key_width), low),
            pltpu.VMEM((heads, owners, shard_rows, index_width), low),
            pltpu.VMEM((turns, owners, shard_rows, key_width), low),
            pltpu.VMEM((turns, owners, shard_rows, index_width), low),
            pltpu.VMEM((side, shard_rows, key_width), low),
            pltpu.VMEM((side, shard_rows, index_width), low),
            sem((5,)),
            sem((side,)),
            sem((side,)),
            sem((side,)),
            sem((side,)),
            sem((owners, turns)),
            sem((owners, turns)),
            sem((turns,)),
            sem((turns,)),
            sem((turns,)),
            sem((turns,)),
            sem((turns,)),
            sem((turns,)),
            sem((side,)),
            sem((side,)),
            sem((side,)),
            sem((side,)),
        ],
        compiler_params=pltpu.CompilerParams(
            collective_id=0, has_side_effects=True, vmem_limit_bytes=VMEM_BYTES
        ),
        name="exchange",
    )(
        queries,
        out_grad,
        latents,
        index_keys,
        index_queries,
        index_weights,
        picked_blocks,
        key_reach.reshape(context // block_rows, block_rows),
    )
    latent_grad, index_key_grad = pl.pallas_call(
        functools.partial(place_kernel, owners),
        out_shape=(
            jax.ShapeDtypeStruct((own_count, shard_rows, key_width), full),
            jax.ShapeDtypeStruct((own_count, shard_rows, index_width), full),
        ),
        in_specs=[pl.BlockSpec(memory_space=pltpu.SMEM), vmem, vmem],
        out_specs=(vmem, vmem),
        compiler_params=pltpu.CompilerParams(vmem_limit_bytes=VMEM_BYTES),
        name="place",
    )(home, back_lat, back_key)
    return (query_grad, latent_grad, iquery_grad, weight_grad, index_key_grad)


def solution(mesh):
    placed = (
        P(("groups", "ctx"), "head", None),
        P(("groups", "ctx"), "head", None),
        P(None, ("groups", "ctx", "head"), None),
        P(None, ("groups", "ctx", "head"), None),
        P(("groups", "ctx"), "head", None),
        P(("groups", "ctx"), "head"),
        P(("groups", "ctx"), None),
        P("groups"),
    )
    return jax.shard_map(
        shards,
        mesh=mesh,
        in_specs=placed,
        out_specs=(
            P(("groups", "ctx"), "head", None),
            P(None, ("groups", "ctx", "head"), None),
            P(("groups", "ctx"), "head", None),
            P(("groups", "ctx"), "head"),
            P(None, ("groups", "ctx", "head"), None),
        ),
        check_vma=False,
    )
```

```python
import functools

import jax
import jax.numpy as jnp
from jax import lax
from jax.experimental import pallas as pl
from jax.experimental.pallas import tpu as pltpu
from jax.sharding import PartitionSpec as P

HEADS = 128
QK_DIM = 192
SCORE_FLOOR = -1e30
LANES = 128
MESH = pl.DeviceIdType.MESH
VMEM_BYTES = 56 * 1024 * 1024

NT = (((1,), (1,)), ((), ()))
TN = (((0,), (0,)), ((), ()))
NN = (((1,), (0,)), ((), ()))


def dot(a, b, dims):
    return lax.dot_general(a, b, dims, preferred_element_type=jnp.float32)


def exchange_kernel(
    owners,
    heads,
    sizes,
    q_hbm,
    g_hbm,
    lat_hbm,
    key_hbm,
    iq_ref,
    iw_ref,
    pick_ref,
    reach_hbm,
    qg_ref,
    back_lat_ref,
    back_key_ref,
    iqg_ref,
    iwg_ref,
    home_ref,
    q_buf,
    g_buf,
    lat_buf,
    key_buf,
    reach_buf,
    want_buf,
    asked,
    row_send,
    rows,
    part,
    glat,
    gkey,
    near_lat,
    near_key,
    mid_lat,
    mid_key,
    far_lat,
    far_key,
    hlat,
    hkey,
    local_sem,
    ask_s,
    ask_r,
    row_s,
    row_r,
    fwd_s,
    fwd_r,
    part_s,
    part_r,
    near_s,
    near_r,
    mid_s,
    mid_r,
    hlat_s,
    hlat_r,
    hkey_s,
    hkey_r,
):
    row_count, local_heads, key_width, latent_width, shard_rows, context = sizes
    key_at = -(-key_width // LANES) * LANES
    block_rows = shard_rows * heads
    shift = owners.bit_length() - 1
    me_c = lax.axis_index("ctx")
    me_h = lax.axis_index("head")
    my_x, my_core = me_h // 2, lax.rem(me_h, 2)
    beside = me_h + 1 - 2 * my_core
    across = lax.rem(me_h + 2, heads)
    opposite = heads - 1 - me_h
    others = (beside, across, opposite)

    def ctx_at(step):
        return lax.rem(me_c + step + owners, owners)

    def remote(src, dst, send_sem, recv_sem, **where):
        return pltpu.make_async_remote_copy(
            src_ref=src,
            dst_ref=dst,
            send_sem=send_sem,
            recv_sem=recv_sem,
            device_id=where,
            device_id_type=MESH,
        )

    sends = []

    def send(copy):
        copy.start()
        sends.append(copy)

    loads = [
        pltpu.make_async_copy(src, dst, local_sem.at[number])
        for number, (src, dst) in enumerate(
            (
                (lat_hbm, lat_buf),
                (key_hbm, key_buf),
                (reach_hbm, reach_buf),
                (q_hbm, q_buf),
                (g_hbm, g_buf),
            )
        )
    ]
    for load in loads:
        load.start()
    barrier = pltpu.get_barrier_semaphore()
    for step in range(1, owners):
        pl.semaphore_signal(
            barrier, inc=1, device_id={"ctx": ctx_at(step)}, device_id_type=MESH
        )
    for other in others:
        pl.semaphore_signal(barrier, inc=1, device_id={"head": other}, device_id_type=MESH)

    lane = lax.broadcasted_iota(jnp.int32, (row_count, LANES), 1)
    diagonal = lax.broadcasted_iota(
        jnp.int32, (row_count, row_count), 0
    ) == lax.broadcasted_iota(jnp.int32, (row_count, row_count), 1)
    by_row = jnp.full((row_count, LANES), -1, jnp.int32)
    for number in range(pick_ref.shape[0]):
        line = jnp.broadcast_to(pick_ref[number : number + 1, :], (row_count, row_count))
        column = jnp.max(jnp.where(diagonal, line, -1), axis=1, keepdims=True)
        column = jnp.broadcast_to(column, (row_count, LANES))
        match = (column >= 0) & ((column & (owners - 1)) == lane)
        by_row = jnp.where(match, column >> shift, by_row)
    wanted = jnp.max(by_row, axis=0, keepdims=True)
    want_buf[...] = jnp.broadcast_to(wanted, want_buf.shape)
    pl.semaphore_wait(barrier, owners + heads - 2)

    asks = []
    for step in range(1, owners):
        asks.append(
            remote(
                want_buf,
                asked.at[step - 1],
                ask_s.at[step - 1],
                ask_r.at[step - 1],
                ctx=ctx_at(step),
            )
        )
        send(asks[-1])

    def hand_on(step, slot_head, number, to):
        slot = rows.at[step, slot_head]
        return remote(slot, slot, fwd_s.at[step, number], fwd_r.at[step, number], head=to)

    loads[0].wait()
    loads[1].wait()
    first_lane = lax.broadcasted_iota(jnp.int32, (1, LANES), 1)
    own_round = jnp.max(jnp.where(first_lane == me_c, wanted, -1))
    at = jnp.maximum(own_round, 0)
    rows[0, me_h, :, :key_width] = lat_buf[at]
    rows[0, me_h, :, key_at:] = key_buf[at]
    homes = [own_round]
    for step in range(1, owners):
        asks[step - 1].wait_recv()
        told = jnp.max(jnp.where(first_lane == me_c, asked[step - 1, 0:1, :], -1))
        homes.append(told)
        at = jnp.maximum(told, 0)
        row_send[step - 1, :, :key_width] = lat_buf[at]
        row_send[step - 1, :, key_at:] = key_buf[at]
        send(
            remote(
                row_send.at[step - 1],
                rows.at[step, me_h],
                row_s.at[step - 1],
                row_r.at[step - 1],
                ctx=ctx_at(-step),
            )
        )
    send(hand_on(0, me_h, 0, across))
    send(hand_on(0, me_h, 1, beside))
    home_lane = lax.broadcasted_iota(jnp.int32, home_ref.shape, 1)
    home_all = jnp.full(home_ref.shape, -1, jnp.int32)
    for step in range(owners):
        home_all = jnp.where(home_lane == step, homes[step], home_all)
    home_ref[...] = home_all

    loads[2].wait()
    first_pos = context - row_count * owners + me_c * row_count
    places = first_pos + lax.broadcasted_iota(jnp.int32, (row_count, block_rows), 0)
    offsets = lax.broadcasted_iota(jnp.int32, (row_count, block_rows), 1)
    seen = []
    for step in range(owners):
        owner = ctx_at(step)
        block = (
            jnp.maximum(jnp.max(jnp.where(first_lane == owner, wanted, -1)), 0) * owners + owner
        )
        ends = jnp.broadcast_to(reach_buf[pl.ds(block, 1), :], places.shape)
        used = jnp.max(jnp.where(lane == owner, by_row, -1), axis=1, keepdims=True)
        used = jnp.broadcast_to(used, places.shape) >= 0
        ok = used & (block * block_rows + offsets <= places) & (places < ends)
        seen.append(jnp.where(ok, 1.0, 0.0))

    loads[3].wait()
    loads[4].wait()
    stack = row_count * local_heads
    queries = q_buf[...].reshape(stack, key_width)
    grads = g_buf[...].reshape(stack, latent_width)
    index_heads, index_width = iq_ref.shape[1], iq_ref.shape[2]
    index_stack = row_count * index_heads
    iqueries = iq_ref[...].reshape(index_stack, index_width)
    eye = jnp.where(
        lax.broadcasted_iota(jnp.int32, (index_heads, index_heads), 0)
        == lax.broadcasted_iota(jnp.int32, (index_heads, index_heads), 1),
        1.0,
        0.0,
    )
    weights = jnp.sum(iw_ref[...][:, None, :] * eye[None], axis=2, keepdims=True)
    score_scale = QK_DIM ** (-0.5)
    index_scores, scores, pulls = [], [], []

    def keys_of(step):
        return rows[step, :, :, :key_width].reshape(block_rows, key_width)

    def ikeys_of(step):
        return rows[step, :, :, key_at:].reshape(block_rows, index_width)

    def multiply(step):
        found = dot(iqueries, ikeys_of(step), NT).reshape(row_count, index_heads, block_rows)
        index_scores.append(found)
        part[me_h, 1, step] = jnp.sum(weights * jnp.maximum(found, 0.0), axis=1)
        keys = keys_of(step)
        found = dot(queries, keys, NT).reshape(row_count, local_heads, block_rows) * score_scale
        scores.append(jnp.where(seen[step][:, None, :] > 0.5, found, SCORE_FLOOR))
        found = dot(grads, keys[:, :latent_width], NT)
        pulls.append(found.reshape(row_count, local_heads, block_rows))

    for turn in range(owners + 2):
        if turn < owners and turn > 0:
            remote(
                row_send.at[0],
                rows.at[turn, me_h],
                row_s.at[turn - 1],
                row_r.at[turn - 1],
                ctx=ctx_at(turn),
            ).wait_recv()
            send(hand_on(turn, me_h, 0, across))
            send(hand_on(turn, me_h, 1, beside))
        if 1 <= turn <= owners:
            hand_on(turn - 1, across, 0, across).wait_recv()
            send(hand_on(turn - 1, across, 2, beside))
        if turn >= 2:
            hand_on(turn - 2, beside, 1, beside).wait_recv()
            hand_on(turn - 2, opposite, 2, beside).wait_recv()
            multiply(turn - 2)

    def share(kind):
        for number, other in enumerate(others):
            slot = part.at[me_h, kind]
            send(remote(slot, slot, part_s.at[kind, number], part_r.at[kind, number], head=other))

    def softmax(chunks):
        top = functools.reduce(jnp.maximum, chunks)
        top = jnp.max(top, axis=-1, keepdims=True)
        raised = [jnp.exp(chunk - top) for chunk in chunks]
        total = jnp.sum(functools.reduce(jnp.add, raised), axis=-1, keepdims=True)
        inverse = 1.0 / total
        return [chunk * inverse for chunk in raised]

    share(1)
    attention = softmax(scores)
    for step in range(owners):
        part[me_h, 0, step] = jnp.sum(attention[step], axis=1)
    share(0)
    inner = functools.reduce(jnp.add, [a * p for a, p in zip(attention, pulls)])
    inner = jnp.sum(inner, axis=-1, keepdims=True)
    order = [*range(1, owners), 0]
    score_grads = [None] * owners
    shape = (heads // 2, 2, shard_rows)
    for step in order:
        found = score_scale * attention[step] * (pulls[step] - inner)
        found = found.astype(jnp.bfloat16).reshape(stack, block_rows)
        score_grads[step] = found
        low = attention[step].astype(jnp.bfloat16).reshape(stack, block_rows)
        key_grad = dot(found, queries, TN)
        value_grad = dot(low, grads, TN)
        front = (key_grad[:, :latent_width] + value_grad).astype(jnp.bfloat16)
        glat[step, :, :, :, :latent_width] = front.reshape(*shape, latent_width)
        rest = key_grad[:, latent_width:].astype(jnp.bfloat16)
        glat[step, :, :, :, latent_width:] = rest.reshape(*shape, key_width - latent_width)
        send(
            remote(
                glat.at[step, :, 1 - my_core],
                near_lat.at[step],
                near_s.at[step],
                near_r.at[step],
                head=beside,
            )
        )

    for kind in range(2):
        for number, other in enumerate(others):
            slot = part.at[other, kind]
            remote(
                slot, slot, part_s.at[kind, number], part_r.at[kind, number], head=other
            ).wait_recv()

    def total_of(kind, step):
        found = part[0, kind, step]
        for head in range(1, heads):
            found = found + part[head, kind, step]
        return found

    logits = [
        jnp.where(seen[step] > 0.5, total_of(1, step), SCORE_FLOOR) for step in range(owners)
    ]
    probs = softmax(logits)
    logit_grads = [probs[step] - total_of(0, step) * (1.0 / HEADS) for step in range(owners)]

    for step in order:
        remote(
            glat.at[step, :, 0],
            near_lat.at[step],
            near_s.at[step],
            near_r.at[step],
            head=beside,
        ).wait_recv()
        total = glat[step, 1 - my_x, my_core].astype(jnp.float32)
        total = total + near_lat[step, 1 - my_x].astype(jnp.float32)
        mid_lat[step] = total.astype(jnp.bfloat16)
        send(
            remote(
                mid_lat.at[step], far_lat.at[step], mid_s.at[step], mid_r.at[step], head=across
            )
        )

    spreads = []
    for step in range(owners):
        found = jnp.where(
            index_scores[step] > 0.0, logit_grads[step][:, None, :] * weights, 0.0
        )
        found = found.astype(jnp.bfloat16).reshape(index_stack, block_rows)
        spreads.append(found)
        found = dot(found, iqueries, TN).astype(jnp.bfloat16)
        gkey[step] = found.reshape(*shape, index_width)
    send(
        remote(
            gkey.at[:, :, 1 - my_core],
            near_key,
            near_s.at[owners],
            near_r.at[owners],
            head=beside,
        )
    )
    found = jnp.zeros((stack, key_width), jnp.float32)
    for step in range(owners):
        found = found + dot(score_grads[step], keys_of(step), NN)
    qg_ref[...] = found.astype(jnp.bfloat16).reshape(row_count, local_heads, key_width)

    remote(
        gkey.at[:, :, 0], near_key, near_s.at[owners], near_r.at[owners], head=beside
    ).wait_recv()
    for step in range(owners):
        total = gkey[step, 1 - my_x, my_core].astype(jnp.float32)
        total = total + near_key[step, 1 - my_x].astype(jnp.float32)
        mid_key[step] = total.astype(jnp.bfloat16)
    send(remote(mid_key, far_key, mid_s.at[owners], mid_r.at[owners], head=across))

    found = jnp.zeros((index_stack, index_width), jnp.float32)
    weight_grad = jnp.zeros((row_count, index_heads, block_rows), jnp.float32)
    for step in range(owners):
        found = found + dot(spreads[step], ikeys_of(step), NN)
        weight_grad = weight_grad + logit_grads[step][:, None, :] * jnp.maximum(
            index_scores[step], 0.0
        )
    iqg_ref[...] = found.astype(jnp.bfloat16).reshape(row_count, index_heads, index_width)
    weight_grad = jnp.sum(weight_grad, axis=-1, keepdims=True)
    iwg_ref[...] = jnp.sum(weight_grad * eye[None], axis=1)

    def home_copy(out, back_ref, out_s, out_r, step):
        return remote(
            out.at[step - 1],
            back_ref.at[step],
            out_s.at[step - 1],
            out_r.at[step - 1],
            ctx=ctx_at(step),
        )

    lat_home = (hlat, back_lat_ref, hlat_s, hlat_r)
    key_home = (hkey, back_key_ref, hkey_s, hkey_r)

    def send_home(own, near, far, home, step):
        total = own[step, my_x, my_core].astype(jnp.float32)
        total = total + near[step, my_x].astype(jnp.float32)
        total = (total + far[step].astype(jnp.float32)).astype(jnp.bfloat16)
        if step == 0:
            home[1][0] = total
        else:
            home[0][step - 1] = total
            send(home_copy(*home, step))

    for step in order:
        remote(
            mid_lat.at[step], far_lat.at[step], mid_s.at[step], mid_r.at[step], head=across
        ).wait_recv()
        send_home(glat, near_lat, far_lat, lat_home, step)
    remote(mid_key, far_key, mid_s.at[owners], mid_r.at[owners], head=across).wait_recv()
    for step in order:
        send_home(gkey, near_key, far_key, key_home, step)
    for home in (lat_home, key_home):
        for step in range(1, owners):
            home_copy(*home, step).wait_recv()
    for copy in sends:
        copy.wait_send()


def place_kernel(
    owners,
    home_ref,
    lat_hbm,
    key_hbm,
    qg_in,
    iqg_in,
    iwg_in,
    lat_out,
    key_out,
    qg_out,
    iqg_out,
    iwg_out,
    lat_buf,
    key_buf,
    sems,
):
    copies = [
        pltpu.make_async_copy(src, dst, sems.at[number])
        for number, (src, dst) in enumerate(
            (
                (lat_hbm, lat_buf),
                (key_hbm, key_buf),
                (qg_in, qg_out),
                (iqg_in, iqg_out),
                (iwg_in, iwg_out),
            )
        )
    ]
    for copy in copies:
        copy.start()
    lat_out[...] = jnp.zeros_like(lat_out)
    key_out[...] = jnp.zeros_like(key_out)
    copies[0].wait()
    copies[1].wait()
    for step in range(owners):
        at = jnp.maximum(home_ref[0, step], 0)
        lat_out[at] = lat_out[at] + lat_buf[step].astype(jnp.float32)
        key_out[at] = key_out[at] + key_buf[step].astype(jnp.float32)
    for copy in copies[2:]:
        copy.wait()


def shards(
    queries, out_grad, latents, index_keys, index_queries, index_weights, picked_blocks, key_reach
):
    owners = lax.axis_size("ctx")
    heads = lax.axis_size("head")
    row_count, local_heads, key_width = queries.shape
    latent_width = out_grad.shape[2]
    own_count, shard_rows = latents.shape[:2]
    index_width = index_keys.shape[2]
    context = key_reach.shape[0]
    block_rows = shard_rows * heads
    wide = -(-key_width // LANES) * LANES + index_width
    sizes = (row_count, local_heads, key_width, latent_width, shard_rows, context)
    low, full, whole = jnp.bfloat16, jnp.float32, jnp.int32
    vmem = pl.BlockSpec(memory_space=pltpu.VMEM)
    anywhere = pl.BlockSpec(memory_space=pl.ANY)
    sem = pltpu.SemaphoreType.DMA
    side = owners - 1
    query_grad, back_lat, back_key, iquery_grad, weight_grad, home = pl.pallas_call(
        functools.partial(exchange_kernel, owners, heads, sizes),
        out_shape=(
            jax.ShapeDtypeStruct(queries.shape, low),
            jax.ShapeDtypeStruct((owners, shard_rows, key_width), low),
            jax.ShapeDtypeStruct((owners, shard_rows, index_width), low),
            jax.ShapeDtypeStruct(index_queries.shape, low),
            jax.ShapeDtypeStruct(index_weights.shape, full),
            jax.ShapeDtypeStruct((8, LANES), whole),
        ),
        in_specs=[anywhere, anywhere, anywhere, anywhere, vmem, vmem, vmem, anywhere],
        out_specs=(vmem,) * 6,
        scratch_shapes=[
            pltpu.VMEM(queries.shape, low),
            pltpu.VMEM(out_grad.shape, low),
            pltpu.VMEM(latents.shape, low),
            pltpu.VMEM(index_keys.shape, low),
            pltpu.VMEM((context // block_rows, block_rows), whole),
            pltpu.VMEM((8, LANES), whole),
            pltpu.VMEM((side, 8, LANES), whole),
            pltpu.VMEM((side, shard_rows, wide), low),
            pltpu.VMEM((owners, heads, shard_rows, wide), low),
            pltpu.VMEM((heads, 2, owners, row_count, block_rows), full),
            pltpu.VMEM((owners, heads // 2, 2, shard_rows, key_width), low),
            pltpu.VMEM((owners, heads // 2, 2, shard_rows, index_width), low),
            pltpu.VMEM((owners, heads // 2, shard_rows, key_width), low),
            pltpu.VMEM((owners, heads // 2, shard_rows, index_width), low),
            pltpu.VMEM((owners, shard_rows, key_width), low),
            pltpu.VMEM((owners, shard_rows, index_width), low),
            pltpu.VMEM((owners, shard_rows, key_width), low),
            pltpu.VMEM((owners, shard_rows, index_width), low),
            pltpu.VMEM((side, shard_rows, key_width), low),
            pltpu.VMEM((side, shard_rows, index_width), low),
            sem((5,)),
            sem((side,)),
            sem((side,)),
            sem((side,)),
            sem((side,)),
            sem((owners, 3)),
            sem((owners, 3)),
            sem((2, 3)),
            sem((2, 3)),
            sem((owners + 1,)),
            sem((owners + 1,)),
            sem((owners + 1,)),
            sem((owners + 1,)),
            sem((side,)),
            sem((side,)),
            sem((side,)),
            sem((side,)),
        ],
        compiler_params=pltpu.CompilerParams(
            collective_id=0, has_side_effects=True, vmem_limit_bytes=VMEM_BYTES
        ),
        name="exchange",
    )(
        queries,
        out_grad,
        latents,
        index_keys,
        index_queries,
        index_weights,
        picked_blocks.T,
        key_reach.reshape(context // block_rows, block_rows),
    )
    latent_grad, index_key_grad, query_grad, iquery_grad, weight_grad = pl.pallas_call(
        functools.partial(place_kernel, owners),
        out_shape=(
            jax.ShapeDtypeStruct((own_count, shard_rows, key_width), full),
            jax.ShapeDtypeStruct((own_count, shard_rows, index_width), full),
            jax.ShapeDtypeStruct(queries.shape, low),
            jax.ShapeDtypeStruct(index_queries.shape, low),
            jax.ShapeDtypeStruct(index_weights.shape, full),
        ),
        in_specs=[pl.BlockSpec(memory_space=pltpu.SMEM)] + [anywhere] * 5,
        out_specs=(vmem, vmem, anywhere, anywhere, anywhere),
        scratch_shapes=[
            pltpu.VMEM(back_lat.shape, low),
            pltpu.VMEM(back_key.shape, low),
            sem((5,)),
        ],
        compiler_params=pltpu.CompilerParams(vmem_limit_bytes=VMEM_BYTES),
        name="place",
    )(home, back_lat, back_key, query_grad, iquery_grad, weight_grad)
    return (query_grad, latent_grad, iquery_grad, weight_grad, index_key_grad)


def solution(mesh):
    placed = (
        P(("groups", "ctx"), "head", None),
        P(("groups", "ctx"), "head", None),
        P(None, ("groups", "ctx", "head"), None),
        P(None, ("groups", "ctx", "head"), None),
        P(("groups", "ctx"), "head", None),
        P(("groups", "ctx"), "head"),
        P(("groups", "ctx"), None),
        P("groups"),
    )
    return jax.shard_map(
        shards,
        mesh=mesh,
        in_specs=placed,
        out_specs=(
            P(("groups", "ctx"), "head", None),
            P(None, ("groups", "ctx", "head"), None),
            P(("groups", "ctx"), "head", None),
            P(("groups", "ctx"), "head"),
            P(None, ("groups", "ctx", "head"), None),
        ),
        check_vma=False,
    )
```

```python
import functools

import jax
import jax.numpy as jnp
from jax import lax
from jax.experimental import pallas as pl
from jax.experimental.pallas import tpu as pltpu
from jax.sharding import PartitionSpec as P

HEADS = 128
QK_DIM = 192
SCORE_FLOOR = -1e30
LANES = 128
MESH = pl.DeviceIdType.MESH
VMEM_BYTES = 56 * 1024 * 1024

NT = (((1,), (1,)), ((), ()))
TN = (((0,), (0,)), ((), ()))
NN = (((1,), (0,)), ((), ()))


def dot(a, b, dims):
    return lax.dot_general(a, b, dims, preferred_element_type=jnp.float32)


def exchange_kernel(
    owners,
    heads,
    sizes,
    q_hbm,
    g_hbm,
    lat_hbm,
    key_hbm,
    iq_ref,
    iw_ref,
    pick_ref,
    reach_hbm,
    qg_ref,
    back_lat_ref,
    back_key_ref,
    iqg_ref,
    iwg_ref,
    home_ref,
    q_buf,
    g_buf,
    lat_buf,
    key_buf,
    reach_buf,
    want_buf,
    asked,
    row_send,
    rows,
    part,
    glat,
    gkey,
    near_lat,
    near_key,
    mid_lat,
    mid_key,
    far_lat,
    far_key,
    hlat,
    hkey,
    local_sem,
    ask_s,
    ask_r,
    row_s,
    row_r,
    fwd_s,
    fwd_r,
    part_s,
    part_r,
    near_s,
    near_r,
    mid_s,
    mid_r,
    hlat_s,
    hlat_r,
    hkey_s,
    hkey_r,
):
    row_count, local_heads, key_width, latent_width, shard_rows, context = sizes
    key_at = -(-key_width // LANES) * LANES
    block_rows = shard_rows * heads
    shift = owners.bit_length() - 1
    me_c = lax.axis_index("ctx")
    me_h = lax.axis_index("head")
    my_x, my_core = me_h // 2, lax.rem(me_h, 2)
    beside = me_h + 1 - 2 * my_core
    across = lax.rem(me_h + 2, heads)
    opposite = heads - 1 - me_h
    others = (beside, across, opposite)

    def ctx_at(step):
        found = me_c
        for bit in range(shift):
            if step >> bit & 1:
                found = found + (1 << bit) * (1 - 2 * lax.rem(me_c // (1 << bit), 2))
        return found

    def remote(src, dst, send_sem, recv_sem, **where):
        return pltpu.make_async_remote_copy(
            src_ref=src,
            dst_ref=dst,
            send_sem=send_sem,
            recv_sem=recv_sem,
            device_id=where,
            device_id_type=MESH,
        )

    sends = []

    def send(copy):
        copy.start()
        sends.append(copy)

    loads = [
        pltpu.make_async_copy(src, dst, local_sem.at[number])
        for number, (src, dst) in enumerate(
            (
                (lat_hbm, lat_buf),
                (key_hbm, key_buf),
                (reach_hbm, reach_buf),
                (q_hbm, q_buf),
                (g_hbm, g_buf),
            )
        )
    ]
    for load in loads:
        load.start()
    barrier = pltpu.get_barrier_semaphore()
    for step in range(1, owners):
        pl.semaphore_signal(
            barrier, inc=1, device_id={"ctx": ctx_at(step)}, device_id_type=MESH
        )
    for other in others:
        pl.semaphore_signal(barrier, inc=1, device_id={"head": other}, device_id_type=MESH)

    lane = lax.broadcasted_iota(jnp.int32, (row_count, LANES), 1)
    diagonal = lax.broadcasted_iota(
        jnp.int32, (row_count, row_count), 0
    ) == lax.broadcasted_iota(jnp.int32, (row_count, row_count), 1)
    by_row = jnp.full((row_count, LANES), -1, jnp.int32)
    for number in range(pick_ref.shape[0]):
        line = jnp.broadcast_to(pick_ref[number : number + 1, :], (row_count, row_count))
        column = jnp.max(jnp.where(diagonal, line, -1), axis=1, keepdims=True)
        column = jnp.broadcast_to(column, (row_count, LANES))
        match = (column >= 0) & ((column & (owners - 1)) == lane)
        by_row = jnp.where(match, column >> shift, by_row)
    wanted = jnp.max(by_row, axis=0, keepdims=True)
    want_buf[...] = jnp.broadcast_to(wanted, want_buf.shape)
    pl.semaphore_wait(barrier, owners + heads - 2)

    asks = []
    for step in range(1, owners):
        asks.append(
            remote(
                want_buf,
                asked.at[step - 1],
                ask_s.at[step - 1],
                ask_r.at[step - 1],
                ctx=ctx_at(step),
            )
        )
        send(asks[-1])

    def hand_on(step, slot_head, number, to):
        slot = rows.at[step, slot_head]
        return remote(slot, slot, fwd_s.at[step, number], fwd_r.at[step, number], head=to)

    loads[0].wait()
    loads[1].wait()
    first_lane = lax.broadcasted_iota(jnp.int32, (1, LANES), 1)
    own_round = jnp.max(jnp.where(first_lane == me_c, wanted, -1))
    at = jnp.maximum(own_round, 0)
    rows[0, me_h, :, :key_width] = lat_buf[at]
    rows[0, me_h, :, key_at:] = key_buf[at]
    homes = [own_round]
    for step in range(1, owners):
        asks[step - 1].wait_recv()
        told = jnp.max(jnp.where(first_lane == me_c, asked[step - 1, 0:1, :], -1))
        homes.append(told)
        at = jnp.maximum(told, 0)
        row_send[step - 1, :, :key_width] = lat_buf[at]
        row_send[step - 1, :, key_at:] = key_buf[at]
        send(
            remote(
                row_send.at[step - 1],
                rows.at[step, me_h],
                row_s.at[step - 1],
                row_r.at[step - 1],
                ctx=ctx_at(step),
            )
        )
    send(hand_on(0, me_h, 0, across))
    send(hand_on(0, me_h, 1, beside))
    home_lane = lax.broadcasted_iota(jnp.int32, home_ref.shape, 1)
    home_all = jnp.full(home_ref.shape, -1, jnp.int32)
    for step in range(owners):
        home_all = jnp.where(home_lane == step, homes[step], home_all)
    home_ref[...] = home_all

    loads[2].wait()
    first_pos = context - row_count * owners + me_c * row_count
    places = first_pos + lax.broadcasted_iota(jnp.int32, (row_count, block_rows), 0)
    offsets = lax.broadcasted_iota(jnp.int32, (row_count, block_rows), 1)
    seen = []
    for step in range(owners):
        owner = ctx_at(step)
        block = (
            jnp.maximum(jnp.max(jnp.where(first_lane == owner, wanted, -1)), 0) * owners + owner
        )
        ends = jnp.broadcast_to(reach_buf[pl.ds(block, 1), :], places.shape)
        used = jnp.max(jnp.where(lane == owner, by_row, -1), axis=1, keepdims=True)
        used = jnp.broadcast_to(used, places.shape) >= 0
        ok = used & (block * block_rows + offsets <= places) & (places < ends)
        seen.append(jnp.where(ok, 1.0, 0.0))

    loads[3].wait()
    loads[4].wait()
    stack = row_count * local_heads
    queries = q_buf[...].reshape(stack, key_width)
    grads = g_buf[...].reshape(stack, latent_width)
    index_heads, index_width = iq_ref.shape[1], iq_ref.shape[2]
    index_stack = row_count * index_heads
    iqueries = iq_ref[...].reshape(index_stack, index_width)
    eye = jnp.where(
        lax.broadcasted_iota(jnp.int32, (index_heads, index_heads), 0)
        == lax.broadcasted_iota(jnp.int32, (index_heads, index_heads), 1),
        1.0,
        0.0,
    )
    weights = jnp.sum(iw_ref[...][:, None, :] * eye[None], axis=2, keepdims=True)
    score_scale = QK_DIM ** (-0.5)
    index_scores, scores, pulls = [], [], []

    def keys_of(step):
        return rows[step, :, :, :key_width].reshape(block_rows, key_width)

    def ikeys_of(step):
        return rows[step, :, :, key_at:].reshape(block_rows, index_width)

    def multiply(step):
        found = dot(iqueries, ikeys_of(step), NT).reshape(row_count, index_heads, block_rows)
        index_scores.append(found)
        part[me_h, 1, step] = jnp.sum(weights * jnp.maximum(found, 0.0), axis=1)
        keys = keys_of(step)
        found = dot(queries, keys, NT).reshape(row_count, local_heads, block_rows) * score_scale
        scores.append(jnp.where(seen[step][:, None, :] > 0.5, found, SCORE_FLOOR))
        found = dot(grads, keys[:, :latent_width], NT)
        pulls.append(found.reshape(row_count, local_heads, block_rows))

    for turn in range(owners + 2):
        if turn < owners and turn > 0:
            remote(
                row_send.at[0],
                rows.at[turn, me_h],
                row_s.at[turn - 1],
                row_r.at[turn - 1],
                ctx=ctx_at(turn),
            ).wait_recv()
            send(hand_on(turn, me_h, 0, across))
            send(hand_on(turn, me_h, 1, beside))
        if 1 <= turn <= owners:
            hand_on(turn - 1, across, 0, across).wait_recv()
            send(hand_on(turn - 1, across, 2, beside))
        if turn >= 2:
            hand_on(turn - 2, beside, 1, beside).wait_recv()
            hand_on(turn - 2, opposite, 2, beside).wait_recv()
            multiply(turn - 2)

    def share(kind):
        for number, other in enumerate(others):
            slot = part.at[me_h, kind]
            send(remote(slot, slot, part_s.at[kind, number], part_r.at[kind, number], head=other))

    def softmax(chunks):
        top = functools.reduce(jnp.maximum, chunks)
        top = jnp.max(top, axis=-1, keepdims=True)
        raised = [jnp.exp(chunk - top) for chunk in chunks]
        total = jnp.sum(functools.reduce(jnp.add, raised), axis=-1, keepdims=True)
        inverse = 1.0 / total
        return [chunk * inverse for chunk in raised]

    share(1)
    attention = softmax(scores)
    for step in range(owners):
        part[me_h, 0, step] = jnp.sum(attention[step], axis=1)
    share(0)
    inner = functools.reduce(jnp.add, [a * p for a, p in zip(attention, pulls)])
    inner = jnp.sum(inner, axis=-1, keepdims=True)
    order = [*range(1, owners), 0]
    score_grads = [None] * owners
    shape = (heads // 2, 2, shard_rows)
    for step in order:
        found = score_scale * attention[step] * (pulls[step] - inner)
        found = found.astype(jnp.bfloat16).reshape(stack, block_rows)
        score_grads[step] = found
        low = attention[step].astype(jnp.bfloat16).reshape(stack, block_rows)
        key_grad = dot(found, queries, TN)
        value_grad = dot(low, grads, TN)
        front = (key_grad[:, :latent_width] + value_grad).astype(jnp.bfloat16)
        glat[step, :, :, :, :latent_width] = front.reshape(*shape, latent_width)
        rest = key_grad[:, latent_width:].astype(jnp.bfloat16)
        glat[step, :, :, :, latent_width:] = rest.reshape(*shape, key_width - latent_width)
        send(
            remote(
                glat.at[step, :, 1 - my_core],
                near_lat.at[step],
                near_s.at[step],
                near_r.at[step],
                head=beside,
            )
        )

    for step in order:
        remote(
            glat.at[step, :, 0],
            near_lat.at[step],
            near_s.at[step],
            near_r.at[step],
            head=beside,
        ).wait_recv()
        total = glat[step, 1 - my_x, my_core].astype(jnp.float32)
        total = total + near_lat[step, 1 - my_x].astype(jnp.float32)
        mid_lat[step] = total.astype(jnp.bfloat16)
        send(
            remote(
                mid_lat.at[step], far_lat.at[step], mid_s.at[step], mid_r.at[step], head=across
            )
        )

    for kind in range(2):
        for number, other in enumerate(others):
            slot = part.at[other, kind]
            remote(
                slot, slot, part_s.at[kind, number], part_r.at[kind, number], head=other
            ).wait_recv()

    def total_of(kind, step):
        found = part[0, kind, step]
        for head in range(1, heads):
            found = found + part[head, kind, step]
        return found

    logits = [
        jnp.where(seen[step] > 0.5, total_of(1, step), SCORE_FLOOR) for step in range(owners)
    ]
    probs = softmax(logits)
    logit_grads = [probs[step] - total_of(0, step) * (1.0 / HEADS) for step in range(owners)]

    spreads = []
    for step in range(owners):
        found = jnp.where(
            index_scores[step] > 0.0, logit_grads[step][:, None, :] * weights, 0.0
        )
        found = found.astype(jnp.bfloat16).reshape(index_stack, block_rows)
        spreads.append(found)
        found = dot(found, iqueries, TN).astype(jnp.bfloat16)
        gkey[step] = found.reshape(*shape, index_width)
    send(
        remote(
            gkey.at[:, :, 1 - my_core],
            near_key,
            near_s.at[owners],
            near_r.at[owners],
            head=beside,
        )
    )
    found = jnp.zeros((stack, key_width), jnp.float32)
    for step in range(owners):
        found = found + dot(score_grads[step], keys_of(step), NN)
    qg_ref[...] = found.astype(jnp.bfloat16).reshape(row_count, local_heads, key_width)

    remote(
        gkey.at[:, :, 0], near_key, near_s.at[owners], near_r.at[owners], head=beside
    ).wait_recv()
    for step in range(owners):
        total = gkey[step, 1 - my_x, my_core].astype(jnp.float32)
        total = total + near_key[step, 1 - my_x].astype(jnp.float32)
        mid_key[step] = total.astype(jnp.bfloat16)
    send(remote(mid_key, far_key, mid_s.at[owners], mid_r.at[owners], head=across))

    found = jnp.zeros((index_stack, index_width), jnp.float32)
    weight_grad = jnp.zeros((row_count, index_heads, block_rows), jnp.float32)
    for step in range(owners):
        found = found + dot(spreads[step], ikeys_of(step), NN)
        weight_grad = weight_grad + logit_grads[step][:, None, :] * jnp.maximum(
            index_scores[step], 0.0
        )
    iqg_ref[...] = found.astype(jnp.bfloat16).reshape(row_count, index_heads, index_width)
    weight_grad = jnp.sum(weight_grad, axis=-1, keepdims=True)
    iwg_ref[...] = jnp.sum(weight_grad * eye[None], axis=1)

    def home_copy(out, back_ref, out_s, out_r, step):
        return remote(
            out.at[step - 1],
            back_ref.at[step],
            out_s.at[step - 1],
            out_r.at[step - 1],
            ctx=ctx_at(step),
        )

    lat_home = (hlat, back_lat_ref, hlat_s, hlat_r)
    key_home = (hkey, back_key_ref, hkey_s, hkey_r)

    def send_home(own, near, far, home, step):
        total = own[step, my_x, my_core].astype(jnp.float32)
        total = total + near[step, my_x].astype(jnp.float32)
        total = (total + far[step].astype(jnp.float32)).astype(jnp.bfloat16)
        if step == 0:
            home[1][0] = total
        else:
            home[0][step - 1] = total
            send(home_copy(*home, step))

    for step in order:
        remote(
            mid_lat.at[step], far_lat.at[step], mid_s.at[step], mid_r.at[step], head=across
        ).wait_recv()
        send_home(glat, near_lat, far_lat, lat_home, step)
    remote(mid_key, far_key, mid_s.at[owners], mid_r.at[owners], head=across).wait_recv()
    for step in order:
        send_home(gkey, near_key, far_key, key_home, step)
    for home in (lat_home, key_home):
        for step in range(1, owners):
            home_copy(*home, step).wait_recv()
    for copy in sends:
        copy.wait_send()


def place_kernel(
    owners,
    home_ref,
    lat_hbm,
    key_hbm,
    qg_in,
    iqg_in,
    iwg_in,
    lat_out,
    key_out,
    qg_out,
    iqg_out,
    iwg_out,
    lat_buf,
    key_buf,
    sems,
):
    copies = [
        pltpu.make_async_copy(src, dst, sems.at[number])
        for number, (src, dst) in enumerate(
            (
                (lat_hbm, lat_buf),
                (key_hbm, key_buf),
                (qg_in, qg_out),
                (iqg_in, iqg_out),
                (iwg_in, iwg_out),
            )
        )
    ]
    for copy in copies:
        copy.start()
    lat_out[...] = jnp.zeros_like(lat_out)
    key_out[...] = jnp.zeros_like(key_out)
    copies[0].wait()
    copies[1].wait()
    for step in range(owners):
        at = jnp.maximum(home_ref[0, step], 0)
        lat_out[at] = lat_out[at] + lat_buf[step].astype(jnp.float32)
        key_out[at] = key_out[at] + key_buf[step].astype(jnp.float32)
    for copy in copies[2:]:
        copy.wait()


def shards(
    queries, out_grad, latents, index_keys, index_queries, index_weights, picked_blocks, key_reach
):
    owners = lax.axis_size("ctx")
    heads = lax.axis_size("head")
    row_count, local_heads, key_width = queries.shape
    latent_width = out_grad.shape[2]
    own_count, shard_rows = latents.shape[:2]
    index_width = index_keys.shape[2]
    context = key_reach.shape[0]
    block_rows = shard_rows * heads
    wide = -(-key_width // LANES) * LANES + index_width
    sizes = (row_count, local_heads, key_width, latent_width, shard_rows, context)
    low, full, whole = jnp.bfloat16, jnp.float32, jnp.int32
    vmem = pl.BlockSpec(memory_space=pltpu.VMEM)
    anywhere = pl.BlockSpec(memory_space=pl.ANY)
    sem = pltpu.SemaphoreType.DMA
    side = owners - 1
    query_grad, back_lat, back_key, iquery_grad, weight_grad, home = pl.pallas_call(
        functools.partial(exchange_kernel, owners, heads, sizes),
        out_shape=(
            jax.ShapeDtypeStruct(queries.shape, low),
            jax.ShapeDtypeStruct((owners, shard_rows, key_width), low),
            jax.ShapeDtypeStruct((owners, shard_rows, index_width), low),
            jax.ShapeDtypeStruct(index_queries.shape, low),
            jax.ShapeDtypeStruct(index_weights.shape, full),
            jax.ShapeDtypeStruct((8, LANES), whole),
        ),
        in_specs=[anywhere, anywhere, anywhere, anywhere, vmem, vmem, vmem, anywhere],
        out_specs=(vmem,) * 6,
        scratch_shapes=[
            pltpu.VMEM(queries.shape, low),
            pltpu.VMEM(out_grad.shape, low),
            pltpu.VMEM(latents.shape, low),
            pltpu.VMEM(index_keys.shape, low),
            pltpu.VMEM((context // block_rows, block_rows), whole),
            pltpu.VMEM((8, LANES), whole),
            pltpu.VMEM((side, 8, LANES), whole),
            pltpu.VMEM((side, shard_rows, wide), low),
            pltpu.VMEM((owners, heads, shard_rows, wide), low),
            pltpu.VMEM((heads, 2, owners, row_count, block_rows), full),
            pltpu.VMEM((owners, heads // 2, 2, shard_rows, key_width), low),
            pltpu.VMEM((owners, heads // 2, 2, shard_rows, index_width), low),
            pltpu.VMEM((owners, heads // 2, shard_rows, key_width), low),
            pltpu.VMEM((owners, heads // 2, shard_rows, index_width), low),
            pltpu.VMEM((owners, shard_rows, key_width), low),
            pltpu.VMEM((owners, shard_rows, index_width), low),
            pltpu.VMEM((owners, shard_rows, key_width), low),
            pltpu.VMEM((owners, shard_rows, index_width), low),
            pltpu.VMEM((side, shard_rows, key_width), low),
            pltpu.VMEM((side, shard_rows, index_width), low),
            sem((5,)),
            sem((side,)),
            sem((side,)),
            sem((side,)),
            sem((side,)),
            sem((owners, 3)),
            sem((owners, 3)),
            sem((2, 3)),
            sem((2, 3)),
            sem((owners + 1,)),
            sem((owners + 1,)),
            sem((owners + 1,)),
            sem((owners + 1,)),
            sem((side,)),
            sem((side,)),
            sem((side,)),
            sem((side,)),
        ],
        compiler_params=pltpu.CompilerParams(
            collective_id=0, has_side_effects=True, vmem_limit_bytes=VMEM_BYTES
        ),
        name="exchange",
    )(
        queries,
        out_grad,
        latents,
        index_keys,
        index_queries,
        index_weights,
        picked_blocks.T,
        key_reach.reshape(context // block_rows, block_rows),
    )
    latent_grad, index_key_grad, query_grad, iquery_grad, weight_grad = pl.pallas_call(
        functools.partial(place_kernel, owners),
        out_shape=(
            jax.ShapeDtypeStruct((own_count, shard_rows, key_width), full),
            jax.ShapeDtypeStruct((own_count, shard_rows, index_width), full),
            jax.ShapeDtypeStruct(queries.shape, low),
            jax.ShapeDtypeStruct(index_queries.shape, low),
            jax.ShapeDtypeStruct(index_weights.shape, full),
        ),
        in_specs=[pl.BlockSpec(memory_space=pltpu.SMEM)] + [anywhere] * 5,
        out_specs=(vmem,) * 5,
        scratch_shapes=[
            pltpu.VMEM(back_lat.shape, low),
            pltpu.VMEM(back_key.shape, low),
            sem((5,)),
        ],
        compiler_params=pltpu.CompilerParams(vmem_limit_bytes=VMEM_BYTES),
        name="place",
    )(home, back_lat, back_key, query_grad, iquery_grad, weight_grad)
    return (query_grad, latent_grad, iquery_grad, weight_grad, index_key_grad)


def solution(mesh):
    placed = (
        P(("groups", "ctx"), "head", None),
        P(("groups", "ctx"), "head", None),
        P(None, ("groups", "ctx", "head"), None),
        P(None, ("groups", "ctx", "head"), None),
        P(("groups", "ctx"), "head", None),
        P(("groups", "ctx"), "head"),
        P(("groups", "ctx"), None),
        P("groups"),
    )
    return jax.shard_map(
        shards,
        mesh=mesh,
        in_specs=placed,
        out_specs=(
            P(("groups", "ctx"), "head", None),
            P(None, ("groups", "ctx", "head"), None),
            P(("groups", "ctx"), "head", None),
            P(("groups", "ctx"), "head"),
            P(None, ("groups", "ctx", "head"), None),
        ),
        check_vma=False,
    )
```

```python
import functools

import jax
import jax.numpy as jnp
from jax import lax
from jax.experimental import pallas as pl
from jax.experimental.pallas import tpu as pltpu
from jax.sharding import PartitionSpec as P

HEADS = 128
QK_DIM = 192
SCORE_FLOOR = -1e30
LANES = 128
MESH = pl.DeviceIdType.MESH
VMEM_BYTES = 56 * 1024 * 1024

NT = (((1,), (1,)), ((), ()))
TN = (((0,), (0,)), ((), ()))
NN = (((1,), (0,)), ((), ()))


def dot(a, b, dims):
    return lax.dot_general(a, b, dims, preferred_element_type=jnp.float32)


def exchange_kernel(
    owners,
    heads,
    sizes,
    q_hbm,
    g_hbm,
    lat_hbm,
    key_hbm,
    iq_ref,
    iw_ref,
    pick_ref,
    reach_hbm,
    qg_ref,
    back_lat_ref,
    back_key_ref,
    iqg_ref,
    iwg_ref,
    home_ref,
    q_buf,
    g_buf,
    lat_buf,
    key_buf,
    reach_buf,
    want_buf,
    asked,
    row_send,
    rows,
    part,
    glat,
    gkey,
    near_lat,
    near_key,
    mid_lat,
    mid_key,
    far_lat,
    far_key,
    hlat,
    hkey,
    local_sem,
    ask_s,
    ask_r,
    row_s,
    row_r,
    fwd_s,
    fwd_r,
    part_s,
    part_r,
    near_s,
    near_r,
    mid_s,
    mid_r,
    hlat_s,
    hlat_r,
    hkey_s,
    hkey_r,
):
    row_count, local_heads, key_width, latent_width, shard_rows, context = sizes
    key_at = -(-key_width // LANES) * LANES
    block_rows = shard_rows * heads
    shift = owners.bit_length() - 1
    me_c = lax.axis_index("ctx")
    me_h = lax.axis_index("head")
    my_x, my_core = me_h // 2, lax.rem(me_h, 2)
    beside = me_h + 1 - 2 * my_core
    across = lax.rem(me_h + 2, heads)
    opposite = heads - 1 - me_h
    others = (beside, across, opposite)

    def ctx_at(step):
        found = me_c
        for bit in range(shift):
            if step >> bit & 1:
                found = found + (1 << bit) * (1 - 2 * lax.rem(me_c // (1 << bit), 2))
        return found

    def remote(src, dst, send_sem, recv_sem, **where):
        return pltpu.make_async_remote_copy(
            src_ref=src,
            dst_ref=dst,
            send_sem=send_sem,
            recv_sem=recv_sem,
            device_id=where,
            device_id_type=MESH,
        )

    sends = []

    def send(copy):
        copy.start()
        sends.append(copy)

    loads = [
        pltpu.make_async_copy(src, dst, local_sem.at[number])
        for number, (src, dst) in enumerate(
            (
                (lat_hbm, lat_buf),
                (key_hbm, key_buf),
                (reach_hbm, reach_buf),
                (q_hbm, q_buf),
                (g_hbm, g_buf),
            )
        )
    ]
    for load in loads:
        load.start()
    barrier = pltpu.get_barrier_semaphore()
    for step in range(1, owners):
        pl.semaphore_signal(
            barrier, inc=1, device_id={"ctx": ctx_at(step)}, device_id_type=MESH
        )
    for other in others:
        pl.semaphore_signal(barrier, inc=1, device_id={"head": other}, device_id_type=MESH)

    lane = lax.broadcasted_iota(jnp.int32, (row_count, LANES), 1)
    diagonal = lax.broadcasted_iota(
        jnp.int32, (row_count, row_count), 0
    ) == lax.broadcasted_iota(jnp.int32, (row_count, row_count), 1)
    by_row = jnp.full((row_count, LANES), -1, jnp.int32)
    for number in range(pick_ref.shape[0]):
        line = jnp.broadcast_to(pick_ref[number : number + 1, :], (row_count, row_count))
        column = jnp.max(jnp.where(diagonal, line, -1), axis=1, keepdims=True)
        column = jnp.broadcast_to(column, (row_count, LANES))
        match = (column >= 0) & ((column & (owners - 1)) == lane)
        by_row = jnp.where(match, column >> shift, by_row)
    wanted = jnp.max(by_row, axis=0, keepdims=True)
    want_buf[...] = jnp.broadcast_to(wanted, want_buf.shape)
    pl.semaphore_wait(barrier, owners + heads - 2)

    asks = []
    for step in range(1, owners):
        asks.append(
            remote(
                want_buf,
                asked.at[step - 1],
                ask_s.at[step - 1],
                ask_r.at[step - 1],
                ctx=ctx_at(step),
            )
        )
        send(asks[-1])

    def hand_on(step, slot_head, number, to):
        slot = rows.at[step, slot_head]
        return remote(slot, slot, fwd_s.at[step, number], fwd_r.at[step, number], head=to)

    loads[0].wait()
    loads[1].wait()
    first_lane = lax.broadcasted_iota(jnp.int32, (1, LANES), 1)
    own_round = jnp.max(jnp.where(first_lane == me_c, wanted, -1))
    at = jnp.maximum(own_round, 0)
    rows[0, me_h, :, :key_width] = lat_buf[at]
    rows[0, me_h, :, key_at:] = key_buf[at]
    homes = [own_round]
    for step in range(1, owners):
        asks[step - 1].wait_recv()
        told = jnp.max(jnp.where(first_lane == me_c, asked[step - 1, 0:1, :], -1))
        homes.append(told)
        at = jnp.maximum(told, 0)
        row_send[step - 1, :, :key_width] = lat_buf[at]
        row_send[step - 1, :, key_at:] = key_buf[at]
        send(
            remote(
                row_send.at[step - 1],
                rows.at[step, me_h],
                row_s.at[step - 1],
                row_r.at[step - 1],
                ctx=ctx_at(step),
            )
        )
    send(hand_on(0, me_h, 0, across))
    send(hand_on(0, me_h, 1, beside))
    home_lane = lax.broadcasted_iota(jnp.int32, home_ref.shape, 1)
    home_all = jnp.full(home_ref.shape, -1, jnp.int32)
    for step in range(owners):
        home_all = jnp.where(home_lane == step, homes[step], home_all)
    home_ref[...] = home_all

    loads[2].wait()
    first_pos = context - row_count * owners + me_c * row_count
    places = first_pos + lax.broadcasted_iota(jnp.int32, (row_count, block_rows), 0)
    offsets = lax.broadcasted_iota(jnp.int32, (row_count, block_rows), 1)
    seen = []
    for step in range(owners):
        owner = ctx_at(step)
        block = (
            jnp.maximum(jnp.max(jnp.where(first_lane == owner, wanted, -1)), 0) * owners + owner
        )
        ends = jnp.broadcast_to(reach_buf[pl.ds(block, 1), :], places.shape)
        used = jnp.max(jnp.where(lane == owner, by_row, -1), axis=1, keepdims=True)
        used = jnp.broadcast_to(used, places.shape) >= 0
        ok = used & (block * block_rows + offsets <= places) & (places < ends)
        seen.append(jnp.where(ok, 1.0, 0.0))

    loads[3].wait()
    loads[4].wait()
    stack = row_count * local_heads
    queries = q_buf[...].reshape(stack, key_width)
    grads = g_buf[...].reshape(stack, latent_width)
    index_heads, index_width = iq_ref.shape[1], iq_ref.shape[2]
    index_stack = row_count * index_heads
    iqueries = iq_ref[...].reshape(index_stack, index_width)
    eye = jnp.where(
        lax.broadcasted_iota(jnp.int32, (index_heads, index_heads), 0)
        == lax.broadcasted_iota(jnp.int32, (index_heads, index_heads), 1),
        1.0,
        0.0,
    )
    weights = jnp.sum(iw_ref[...][:, None, :] * eye[None], axis=2, keepdims=True)
    score_scale = QK_DIM ** (-0.5)
    index_scores, scores, pulls = [], [], []

    def keys_of(step):
        return rows[step, :, :, :key_width].reshape(block_rows, key_width)

    def ikeys_of(step):
        return rows[step, :, :, key_at:].reshape(block_rows, index_width)

    def multiply(step):
        found = dot(iqueries, ikeys_of(step), NT).reshape(row_count, index_heads, block_rows)
        index_scores.append(found)
        part[me_h, 1, step] = jnp.sum(weights * jnp.maximum(found, 0.0), axis=1)
        keys = keys_of(step)
        found = dot(queries, keys, NT).reshape(row_count, local_heads, block_rows) * score_scale
        scores.append(jnp.where(seen[step][:, None, :] > 0.5, found, SCORE_FLOOR))
        found = dot(grads, keys[:, :latent_width], NT)
        pulls.append(found.reshape(row_count, local_heads, block_rows))

    for turn in range(owners + 2):
        if turn < owners and turn > 0:
            remote(
                row_send.at[0],
                rows.at[turn, me_h],
                row_s.at[turn - 1],
                row_r.at[turn - 1],
                ctx=ctx_at(turn),
            ).wait_recv()
            send(hand_on(turn, me_h, 0, across))
            send(hand_on(turn, me_h, 1, beside))
        if 1 <= turn <= owners:
            hand_on(turn - 1, across, 0, across).wait_recv()
            send(hand_on(turn - 1, across, 2, beside))
        if turn >= 2:
            hand_on(turn - 2, beside, 1, beside).wait_recv()
            hand_on(turn - 2, opposite, 2, beside).wait_recv()
            multiply(turn - 2)

    def share(kind):
        for number, other in enumerate(others):
            slot = part.at[me_h, kind]
            send(remote(slot, slot, part_s.at[kind, number], part_r.at[kind, number], head=other))

    def softmax(chunks):
        top = functools.reduce(jnp.maximum, chunks)
        top = jnp.max(top, axis=-1, keepdims=True)
        raised = [jnp.exp(chunk - top) for chunk in chunks]
        total = jnp.sum(functools.reduce(jnp.add, raised), axis=-1, keepdims=True)
        inverse = 1.0 / total
        return [chunk * inverse for chunk in raised]

    share(1)
    attention = softmax(scores)
    for step in range(owners):
        part[me_h, 0, step] = jnp.sum(attention[step], axis=1)
    share(0)
    inner = functools.reduce(jnp.add, [a * p for a, p in zip(attention, pulls)])
    inner = jnp.sum(inner, axis=-1, keepdims=True)
    order = [*range(1, owners), 0]
    score_grads = [None] * owners
    shape = (heads // 2, 2, shard_rows)
    for step in order:
        found = score_scale * attention[step] * (pulls[step] - inner)
        found = found.astype(jnp.bfloat16).reshape(stack, block_rows)
        score_grads[step] = found
        low = attention[step].astype(jnp.bfloat16).reshape(stack, block_rows)
        key_grad = dot(found, queries, TN)
        value_grad = dot(low, grads, TN)
        front = (key_grad[:, :latent_width] + value_grad).astype(jnp.bfloat16)
        glat[step, :, :, :, :latent_width] = front.reshape(*shape, latent_width)
        rest = key_grad[:, latent_width:].astype(jnp.bfloat16)
        glat[step, :, :, :, latent_width:] = rest.reshape(*shape, key_width - latent_width)
        send(
            remote(
                glat.at[step, :, 1 - my_core],
                near_lat.at[step],
                near_s.at[step],
                near_r.at[step],
                head=beside,
            )
        )

    found = jnp.zeros((stack, key_width), jnp.float32)
    for step in range(owners):
        found = found + dot(score_grads[step], keys_of(step), NN)
    qg_ref[...] = found.astype(jnp.bfloat16).reshape(row_count, local_heads, key_width)

    for step in order:
        remote(
            glat.at[step, :, 0],
            near_lat.at[step],
            near_s.at[step],
            near_r.at[step],
            head=beside,
        ).wait_recv()
        total = glat[step, 1 - my_x, my_core].astype(jnp.float32)
        total = total + near_lat[step, 1 - my_x].astype(jnp.float32)
        mid_lat[step] = total.astype(jnp.bfloat16)
        send(
            remote(
                mid_lat.at[step], far_lat.at[step], mid_s.at[step], mid_r.at[step], head=across
            )
        )

    for kind in range(2):
        for number, other in enumerate(others):
            slot = part.at[other, kind]
            remote(
                slot, slot, part_s.at[kind, number], part_r.at[kind, number], head=other
            ).wait_recv()

    def total_of(kind, step):
        found = part[0, kind, step]
        for head in range(1, heads):
            found = found + part[head, kind, step]
        return found

    logits = [
        jnp.where(seen[step] > 0.5, total_of(1, step), SCORE_FLOOR) for step in range(owners)
    ]
    probs = softmax(logits)
    logit_grads = [probs[step] - total_of(0, step) * (1.0 / HEADS) for step in range(owners)]

    spreads = []
    for step in range(owners):
        found = jnp.where(
            index_scores[step] > 0.0, logit_grads[step][:, None, :] * weights, 0.0
        )
        found = found.astype(jnp.bfloat16).reshape(index_stack, block_rows)
        spreads.append(found)
        found = dot(found, iqueries, TN).astype(jnp.bfloat16)
        gkey[step] = found.reshape(*shape, index_width)
    send(
        remote(
            gkey.at[:, :, 1 - my_core],
            near_key,
            near_s.at[owners],
            near_r.at[owners],
            head=beside,
        )
    )
    remote(
        gkey.at[:, :, 0], near_key, near_s.at[owners], near_r.at[owners], head=beside
    ).wait_recv()
    for step in range(owners):
        total = gkey[step, 1 - my_x, my_core].astype(jnp.float32)
        total = total + near_key[step, 1 - my_x].astype(jnp.float32)
        mid_key[step] = total.astype(jnp.bfloat16)
    send(remote(mid_key, far_key, mid_s.at[owners], mid_r.at[owners], head=across))

    found = jnp.zeros((index_stack, index_width), jnp.float32)
    weight_grad = jnp.zeros((row_count, index_heads, block_rows), jnp.float32)
    for step in range(owners):
        found = found + dot(spreads[step], ikeys_of(step), NN)
        weight_grad = weight_grad + logit_grads[step][:, None, :] * jnp.maximum(
            index_scores[step], 0.0
        )
    iqg_ref[...] = found.astype(jnp.bfloat16).reshape(row_count, index_heads, index_width)
    weight_grad = jnp.sum(weight_grad, axis=-1, keepdims=True)
    iwg_ref[...] = jnp.sum(weight_grad * eye[None], axis=1)

    def home_copy(out, back_ref, out_s, out_r, step):
        return remote(
            out.at[step - 1],
            back_ref.at[step],
            out_s.at[step - 1],
            out_r.at[step - 1],
            ctx=ctx_at(step),
        )

    lat_home = (hlat, back_lat_ref, hlat_s, hlat_r)
    key_home = (hkey, back_key_ref, hkey_s, hkey_r)

    def send_home(own, near, far, home, step):
        total = own[step, my_x, my_core].astype(jnp.float32)
        total = total + near[step, my_x].astype(jnp.float32)
        total = (total + far[step].astype(jnp.float32)).astype(jnp.bfloat16)
        if step == 0:
            home[1][0] = total
        else:
            home[0][step - 1] = total
            send(home_copy(*home, step))

    for step in order:
        remote(
            mid_lat.at[step], far_lat.at[step], mid_s.at[step], mid_r.at[step], head=across
        ).wait_recv()
        send_home(glat, near_lat, far_lat, lat_home, step)
    remote(mid_key, far_key, mid_s.at[owners], mid_r.at[owners], head=across).wait_recv()
    for step in order:
        send_home(gkey, near_key, far_key, key_home, step)
    for home in (lat_home, key_home):
        for step in range(1, owners):
            home_copy(*home, step).wait_recv()
    for copy in sends:
        copy.wait_send()


def place_kernel(
    owners,
    home_ref,
    lat_ref,
    key_ref,
    qg_in,
    iqg_in,
    iwg_in,
    lat_out,
    key_out,
    qg_out,
    iqg_out,
    iwg_out,
    lat_buf,
    key_buf,
    small_sem,
    part_sem,
):
    copies = [
        pltpu.make_async_copy(src, dst, small_sem.at[number])
        for number, (src, dst) in enumerate(
            ((qg_in, qg_out), (iqg_in, iqg_out), (iwg_in, iwg_out))
        )
    ]
    for copy in copies:
        copy.start()
    lane = lax.broadcasted_iota(jnp.int32, (1, LANES), 1)
    told = home_ref[0:1, :]
    homes = [jnp.max(jnp.where(lane == step, told, 0)) for step in range(owners)]
    parts = part_sem.shape[1]
    span = lat_buf.shape[0] // parts
    for part in range(parts):
        here = pl.ds(part * span, span)
        lat_buf[here] = jnp.zeros((span, *lat_buf.shape[1:]), jnp.float32)
        key_buf[here] = jnp.zeros((span, *key_buf.shape[1:]), jnp.float32)
        for step in range(owners):
            at = homes[step]

            @pl.when((at >= part * span) & (at < (part + 1) * span))
            def _():
                lat_buf[at] = lat_buf[at] + lat_ref[step].astype(jnp.float32)
                key_buf[at] = key_buf[at] + key_ref[step].astype(jnp.float32)

        for kind, (buf, out) in enumerate(((lat_buf, lat_out), (key_buf, key_out))):
            copies.append(
                pltpu.make_async_copy(buf.at[here], out.at[here], part_sem.at[kind, part])
            )
            copies[-1].start()
    for copy in copies:
        copy.wait()


def shards(
    queries, out_grad, latents, index_keys, index_queries, index_weights, picked_blocks, key_reach
):
    owners = lax.axis_size("ctx")
    heads = lax.axis_size("head")
    row_count, local_heads, key_width = queries.shape
    latent_width = out_grad.shape[2]
    own_count, shard_rows = latents.shape[:2]
    index_width = index_keys.shape[2]
    context = key_reach.shape[0]
    block_rows = shard_rows * heads
    wide = -(-key_width // LANES) * LANES + index_width
    sizes = (row_count, local_heads, key_width, latent_width, shard_rows, context)
    low, full, whole = jnp.bfloat16, jnp.float32, jnp.int32
    vmem = pl.BlockSpec(memory_space=pltpu.VMEM)
    anywhere = pl.BlockSpec(memory_space=pl.ANY)
    sem = pltpu.SemaphoreType.DMA
    side = owners - 1
    query_grad, back_lat, back_key, iquery_grad, weight_grad, home = pl.pallas_call(
        functools.partial(exchange_kernel, owners, heads, sizes),
        out_shape=(
            pltpu.VMEM(queries.shape, low),
            pltpu.VMEM((owners, shard_rows, key_width), low),
            pltpu.VMEM((owners, shard_rows, index_width), low),
            pltpu.VMEM(index_queries.shape, low),
            pltpu.VMEM(index_weights.shape, full),
            pltpu.VMEM((8, LANES), whole),
        ),
        in_specs=[anywhere, anywhere, anywhere, anywhere, vmem, vmem, vmem, anywhere],
        out_specs=(vmem,) * 6,
        scratch_shapes=[
            pltpu.VMEM(queries.shape, low),
            pltpu.VMEM(out_grad.shape, low),
            pltpu.VMEM(latents.shape, low),
            pltpu.VMEM(index_keys.shape, low),
            pltpu.VMEM((context // block_rows, block_rows), whole),
            pltpu.VMEM((8, LANES), whole),
            pltpu.VMEM((side, 8, LANES), whole),
            pltpu.VMEM((side, shard_rows, wide), low),
            pltpu.VMEM((owners, heads, shard_rows, wide), low),
            pltpu.VMEM((heads, 2, owners, row_count, block_rows), full),
            pltpu.VMEM((owners, heads // 2, 2, shard_rows, key_width), low),
            pltpu.VMEM((owners, heads // 2, 2, shard_rows, index_width), low),
            pltpu.VMEM((owners, heads // 2, shard_rows, key_width), low),
            pltpu.VMEM((owners, heads // 2, shard_rows, index_width), low),
            pltpu.VMEM((owners, shard_rows, key_width), low),
            pltpu.VMEM((owners, shard_rows, index_width), low),
            pltpu.VMEM((owners, shard_rows, key_width), low),
            pltpu.VMEM((owners, shard_rows, index_width), low),
            pltpu.VMEM((side, shard_rows, key_width), low),
            pltpu.VMEM((side, shard_rows, index_width), low),
            sem((5,)),
            sem((side,)),
            sem((side,)),
            sem((side,)),
            sem((side,)),
            sem((owners, 3)),
            sem((owners, 3)),
            sem((2, 3)),
            sem((2, 3)),
            sem((owners + 1,)),
            sem((owners + 1,)),
            sem((owners + 1,)),
            sem((owners + 1,)),
            sem((side,)),
            sem((side,)),
            sem((side,)),
            sem((side,)),
        ],
        compiler_params=pltpu.CompilerParams(
            collective_id=0, has_side_effects=True, vmem_limit_bytes=VMEM_BYTES
        ),
        name="exchange",
    )(
        queries,
        out_grad,
        latents,
        index_keys,
        index_queries,
        index_weights,
        picked_blocks.T,
        key_reach.reshape(context // block_rows, block_rows),
    )
    latent_grad, index_key_grad, query_grad, iquery_grad, weight_grad = pl.pallas_call(
        functools.partial(place_kernel, owners),
        out_shape=(
            jax.ShapeDtypeStruct((own_count, shard_rows, key_width), full),
            jax.ShapeDtypeStruct((own_count, shard_rows, index_width), full),
            jax.ShapeDtypeStruct(queries.shape, low),
            jax.ShapeDtypeStruct(index_queries.shape, low),
            jax.ShapeDtypeStruct(index_weights.shape, full),
        ),
        in_specs=[vmem] * 6,
        out_specs=(anywhere,) * 5,
        scratch_shapes=[
            pltpu.VMEM((own_count, shard_rows, key_width), full),
            pltpu.VMEM((own_count, shard_rows, index_width), full),
            sem((3,)),
            sem((2, 4)),
        ],
        compiler_params=pltpu.CompilerParams(vmem_limit_bytes=VMEM_BYTES),
        name="place",
    )(
        *(
            pltpu.with_memory_space_constraint(found, pltpu.VMEM)
            for found in (home, back_lat, back_key, query_grad, iquery_grad, weight_grad)
        )
    )
    return (query_grad, latent_grad, iquery_grad, weight_grad, index_key_grad)


def solution(mesh):
    placed = (
        P(("groups", "ctx"), "head", None),
        P(("groups", "ctx"), "head", None),
        P(None, ("groups", "ctx", "head"), None),
        P(None, ("groups", "ctx", "head"), None),
        P(("groups", "ctx"), "head", None),
        P(("groups", "ctx"), "head"),
        P(("groups", "ctx"), None),
        P("groups"),
    )
    return jax.shard_map(
        shards,
        mesh=mesh,
        in_specs=placed,
        out_specs=(
            P(("groups", "ctx"), "head", None),
            P(None, ("groups", "ctx", "head"), None),
            P(("groups", "ctx"), "head", None),
            P(("groups", "ctx"), "head"),
            P(None, ("groups", "ctx", "head"), None),
        ),
        check_vma=False,
    )
```

```python
import functools

import jax
import jax.numpy as jnp
from jax import lax
from jax.experimental import pallas as pl
from jax.experimental.pallas import tpu as pltpu
from jax.sharding import PartitionSpec as P

HEADS = 128
QK_DIM = 192
SCORE_FLOOR = -1e30
LANES = 128
MESH = pl.DeviceIdType.MESH
VMEM_BYTES = 56 * 1024 * 1024

NT = (((1,), (1,)), ((), ()))
TN = (((0,), (0,)), ((), ()))
NN = (((1,), (0,)), ((), ()))


def dot(a, b, dims):
    return lax.dot_general(a, b, dims, preferred_element_type=jnp.float32)


def exchange_kernel(
    owners,
    heads,
    sizes,
    q_hbm,
    g_hbm,
    lat_hbm,
    key_hbm,
    iq_hbm,
    iw_hbm,
    pick_hbm,
    reach_hbm,
    qg_ref,
    back_lat_ref,
    back_key_ref,
    iqg_ref,
    iwg_ref,
    home_ref,
    iq_ref,
    iw_ref,
    pick_ref,
    q_buf,
    g_buf,
    lat_buf,
    key_buf,
    reach_buf,
    want_buf,
    asked,
    row_send,
    rows,
    part,
    glat,
    gkey,
    near_lat,
    near_key,
    mid_lat,
    mid_key,
    far_lat,
    far_key,
    hlat,
    hkey,
    local_sem,
    ask_s,
    ask_r,
    row_s,
    row_r,
    fwd_s,
    fwd_r,
    part_s,
    part_r,
    near_s,
    near_r,
    mid_s,
    mid_r,
    hlat_s,
    hlat_r,
    hkey_s,
    hkey_r,
):
    row_count, local_heads, key_width, latent_width, shard_rows, context = sizes
    key_at = -(-key_width // LANES) * LANES
    block_rows = shard_rows * heads
    shift = owners.bit_length() - 1
    me_c = lax.axis_index("ctx")
    me_h = lax.axis_index("head")
    my_x, my_core = me_h // 2, lax.rem(me_h, 2)
    beside = me_h + 1 - 2 * my_core
    across = lax.rem(me_h + 2, heads)
    opposite = heads - 1 - me_h
    others = (beside, across, opposite)

    def ctx_at(step):
        found = me_c
        for bit in range(shift):
            if step >> bit & 1:
                found = found + (1 << bit) * (1 - 2 * lax.rem(me_c // (1 << bit), 2))
        return found

    def remote(src, dst, send_sem, recv_sem, **where):
        return pltpu.make_async_remote_copy(
            src_ref=src,
            dst_ref=dst,
            send_sem=send_sem,
            recv_sem=recv_sem,
            device_id=where,
            device_id_type=MESH,
        )

    sends = []

    def send(copy):
        copy.start()
        sends.append(copy)

    loads = [
        pltpu.make_async_copy(src, dst, local_sem.at[number])
        for number, (src, dst) in enumerate(
            (
                (lat_hbm, lat_buf),
                (key_hbm, key_buf),
                (reach_hbm, reach_buf),
                (q_hbm, q_buf),
                (g_hbm, g_buf),
                (iq_hbm, iq_ref),
                (iw_hbm, iw_ref),
                (pick_hbm, pick_ref),
            )
        )
    ]
    barrier = pltpu.get_barrier_semaphore()
    for step in range(1, owners):
        pl.semaphore_signal(
            barrier, inc=1, device_id={"ctx": ctx_at(step)}, device_id_type=MESH
        )
    for other in others:
        pl.semaphore_signal(barrier, inc=1, device_id={"head": other}, device_id_type=MESH)
    for load in (loads[7], *loads[:7]):
        load.start()
    loads[7].wait()

    lane = lax.broadcasted_iota(jnp.int32, (row_count, LANES), 1)
    diagonal = lax.broadcasted_iota(
        jnp.int32, (row_count, row_count), 0
    ) == lax.broadcasted_iota(jnp.int32, (row_count, row_count), 1)
    by_row = jnp.full((row_count, LANES), -1, jnp.int32)
    for number in range(pick_ref.shape[0]):
        line = jnp.broadcast_to(pick_ref[number : number + 1, :], (row_count, row_count))
        column = jnp.max(jnp.where(diagonal, line, -1), axis=1, keepdims=True)
        column = jnp.broadcast_to(column, (row_count, LANES))
        match = (column >= 0) & ((column & (owners - 1)) == lane)
        by_row = jnp.where(match, column >> shift, by_row)
    wanted = jnp.max(by_row, axis=0, keepdims=True)
    want_buf[...] = jnp.broadcast_to(wanted, want_buf.shape)
    pl.semaphore_wait(barrier, owners + heads - 2)

    asks = []
    for step in range(1, owners):
        asks.append(
            remote(
                want_buf,
                asked.at[step - 1],
                ask_s.at[step - 1],
                ask_r.at[step - 1],
                ctx=ctx_at(step),
            )
        )
        send(asks[-1])

    def hand_across(step, x):
        slot = rows.at[step, x, my_core]
        return remote(slot, slot, fwd_s.at[step, 0], fwd_r.at[step, 0], head=across)

    def hand_beside(step, core):
        slot = rows.at[step, :, core]
        return remote(slot, slot, fwd_s.at[step, 1], fwd_r.at[step, 1], head=beside)

    loads[0].wait()
    loads[1].wait()
    first_lane = lax.broadcasted_iota(jnp.int32, (1, LANES), 1)
    own_round = jnp.max(jnp.where(first_lane == me_c, wanted, -1))
    at = jnp.maximum(own_round, 0)
    rows[0, my_x, my_core, :, :key_width] = lat_buf[at]
    rows[0, my_x, my_core, :, key_at:] = key_buf[at]
    homes = [own_round]
    for step in range(1, owners):
        asks[step - 1].wait_recv()
        told = jnp.max(jnp.where(first_lane == me_c, asked[step - 1, 0:1, :], -1))
        homes.append(told)
        at = jnp.maximum(told, 0)
        row_send[step - 1, :, :key_width] = lat_buf[at]
        row_send[step - 1, :, key_at:] = key_buf[at]
        send(
            remote(
                row_send.at[step - 1],
                rows.at[step, my_x, my_core],
                row_s.at[step - 1],
                row_r.at[step - 1],
                ctx=ctx_at(step),
            )
        )
    send(hand_across(0, my_x))
    home_lane = lax.broadcasted_iota(jnp.int32, home_ref.shape, 1)
    home_all = jnp.full(home_ref.shape, -1, jnp.int32)
    for step in range(owners):
        home_all = jnp.where(home_lane == step, homes[step], home_all)
    home_ref[...] = home_all

    loads[2].wait()
    first_pos = context - row_count * owners + me_c * row_count
    places = first_pos + lax.broadcasted_iota(jnp.int32, (row_count, block_rows), 0)
    offsets = lax.broadcasted_iota(jnp.int32, (row_count, block_rows), 1)
    seen = []
    for step in range(owners):
        owner = ctx_at(step)
        block = (
            jnp.maximum(jnp.max(jnp.where(first_lane == owner, wanted, -1)), 0) * owners + owner
        )
        ends = jnp.broadcast_to(reach_buf[pl.ds(block, 1), :], places.shape)
        used = jnp.max(jnp.where(lane == owner, by_row, -1), axis=1, keepdims=True)
        used = jnp.broadcast_to(used, places.shape) >= 0
        ok = used & (block * block_rows + offsets <= places) & (places < ends)
        seen.append(jnp.where(ok, 1.0, 0.0))

    for load in loads[3:7]:
        load.wait()
    stack = row_count * local_heads
    queries = q_buf[...].reshape(stack, key_width)
    grads = g_buf[...].reshape(stack, latent_width)
    index_heads, index_width = iq_ref.shape[1], iq_ref.shape[2]
    index_stack = row_count * index_heads
    iqueries = iq_ref[...].reshape(index_stack, index_width)
    eye = jnp.where(
        lax.broadcasted_iota(jnp.int32, (index_heads, index_heads), 0)
        == lax.broadcasted_iota(jnp.int32, (index_heads, index_heads), 1),
        1.0,
        0.0,
    )
    weights = jnp.sum(iw_ref[...][:, None, :] * eye[None], axis=2, keepdims=True)
    score_scale = QK_DIM ** (-0.5)
    index_scores, scores, pulls = [], [], []

    def keys_of(step):
        return rows[step, :, :, :, :key_width].reshape(block_rows, key_width)

    def ikeys_of(step):
        return rows[step, :, :, :, key_at:].reshape(block_rows, index_width)

    def multiply(step):
        found = dot(iqueries, ikeys_of(step), NT).reshape(row_count, index_heads, block_rows)
        index_scores.append(found)
        part[me_h, 1, step] = jnp.sum(weights * jnp.maximum(found, 0.0), axis=1)
        keys = keys_of(step)
        found = dot(queries, keys, NT).reshape(row_count, local_heads, block_rows) * score_scale
        scores.append(jnp.where(seen[step][:, None, :] > 0.5, found, SCORE_FLOOR))
        found = dot(grads, keys[:, :latent_width], NT)
        pulls.append(found.reshape(row_count, local_heads, block_rows))

    for turn in range(owners + 2):
        if turn < owners and turn > 0:
            remote(
                row_send.at[0],
                rows.at[turn, my_x, my_core],
                row_s.at[turn - 1],
                row_r.at[turn - 1],
                ctx=ctx_at(turn),
            ).wait_recv()
            send(hand_across(turn, my_x))
        if 1 <= turn <= owners:
            hand_across(turn - 1, 1 - my_x).wait_recv()
            send(hand_beside(turn - 1, my_core))
        if turn >= 2:
            hand_beside(turn - 2, 1 - my_core).wait_recv()
            multiply(turn - 2)

    def share(kind):
        for number, other in enumerate(others):
            slot = part.at[me_h, kind]
            send(remote(slot, slot, part_s.at[kind, number], part_r.at[kind, number], head=other))

    def softmax(chunks):
        top = functools.reduce(jnp.maximum, chunks)
        top = jnp.max(top, axis=-1, keepdims=True)
        raised = [jnp.exp(chunk - top) for chunk in chunks]
        total = jnp.sum(functools.reduce(jnp.add, raised), axis=-1, keepdims=True)
        inverse = 1.0 / total
        return [chunk * inverse for chunk in raised]

    share(1)
    attention = softmax(scores)
    for step in range(owners):
        part[me_h, 0, step] = jnp.sum(attention[step], axis=1)
    share(0)
    inner = functools.reduce(jnp.add, [a * p for a, p in zip(attention, pulls)])
    inner = jnp.sum(inner, axis=-1, keepdims=True)
    order = [first + more for first in range(owners - 2, -1, -2) for more in range(2)]

    def near_copy(first):
        two = pl.ds(first, 2)
        return remote(
            glat.at[two, :, 1 - my_core],
            near_lat.at[two],
            near_s.at[first],
            near_r.at[first],
            head=beside,
        )

    def mid_copy(first):
        two = pl.ds(first, 2)
        return remote(
            mid_lat.at[two], far_lat.at[two], mid_s.at[first], mid_r.at[first], head=across
        )

    score_grads = [None] * owners
    shape = (heads // 2, 2, shard_rows)
    for step in order:
        found = score_scale * attention[step] * (pulls[step] - inner)
        found = found.astype(jnp.bfloat16).reshape(stack, block_rows)
        score_grads[step] = found
        low = attention[step].astype(jnp.bfloat16).reshape(stack, block_rows)
        key_grad = dot(found, queries, TN)
        value_grad = dot(low, grads, TN)
        front = (key_grad[:, :latent_width] + value_grad).astype(jnp.bfloat16)
        glat[step, :, :, :, :latent_width] = front.reshape(*shape, latent_width)
        rest = key_grad[:, latent_width:].astype(jnp.bfloat16)
        glat[step, :, :, :, latent_width:] = rest.reshape(*shape, key_width - latent_width)
        if step % 2:
            send(near_copy(step - 1))

    found = jnp.zeros((stack, key_width), jnp.float32)
    for step in range(owners):
        found = found + dot(score_grads[step], keys_of(step), NN)
    qg_ref[...] = found.astype(jnp.bfloat16).reshape(row_count, local_heads, key_width)

    for step in order:
        if step % 2 == 0:
            near_copy(step).wait_recv()
        total = glat[step, 1 - my_x, my_core].astype(jnp.float32)
        total = total + near_lat[step, 1 - my_x].astype(jnp.float32)
        mid_lat[step] = total.astype(jnp.bfloat16)
        if step % 2:
            send(mid_copy(step - 1))

    for kind in range(2):
        for number, other in enumerate(others):
            slot = part.at[other, kind]
            remote(
                slot, slot, part_s.at[kind, number], part_r.at[kind, number], head=other
            ).wait_recv()

    def total_of(kind, step):
        found = part[0, kind, step]
        for head in range(1, heads):
            found = found + part[head, kind, step]
        return found

    logits = [
        jnp.where(seen[step] > 0.5, total_of(1, step), SCORE_FLOOR) for step in range(owners)
    ]
    probs = softmax(logits)
    logit_grads = [probs[step] - total_of(0, step) * (1.0 / HEADS) for step in range(owners)]

    spreads = []
    for step in range(owners):
        found = jnp.where(
            index_scores[step] > 0.0, logit_grads[step][:, None, :] * weights, 0.0
        )
        found = found.astype(jnp.bfloat16).reshape(index_stack, block_rows)
        spreads.append(found)
        found = dot(found, iqueries, TN).astype(jnp.bfloat16)
        gkey[step] = found.reshape(*shape, index_width)
    send(
        remote(
            gkey.at[:, :, 1 - my_core],
            near_key,
            near_s.at[owners],
            near_r.at[owners],
            head=beside,
        )
    )
    remote(
        gkey.at[:, :, 0], near_key, near_s.at[owners], near_r.at[owners], head=beside
    ).wait_recv()
    for step in range(owners):
        total = gkey[step, 1 - my_x, my_core].astype(jnp.float32)
        total = total + near_key[step, 1 - my_x].astype(jnp.float32)
        mid_key[step] = total.astype(jnp.bfloat16)
    send(remote(mid_key, far_key, mid_s.at[owners], mid_r.at[owners], head=across))

    found = jnp.zeros((index_stack, index_width), jnp.float32)
    weight_grad = jnp.zeros((row_count, index_heads, block_rows), jnp.float32)
    for step in range(owners):
        found = found + dot(spreads[step], ikeys_of(step), NN)
        weight_grad = weight_grad + logit_grads[step][:, None, :] * jnp.maximum(
            index_scores[step], 0.0
        )
    iqg_ref[...] = found.astype(jnp.bfloat16).reshape(row_count, index_heads, index_width)
    weight_grad = jnp.sum(weight_grad, axis=-1, keepdims=True)
    iwg_ref[...] = jnp.sum(weight_grad * eye[None], axis=1)

    def home_copy(out, back_ref, out_s, out_r, step):
        return remote(
            out.at[step - 1],
            back_ref.at[step],
            out_s.at[step - 1],
            out_r.at[step - 1],
            ctx=ctx_at(step),
        )

    lat_home = (hlat, back_lat_ref, hlat_s, hlat_r)
    key_home = (hkey, back_key_ref, hkey_s, hkey_r)

    def send_home(own, near, far, home, step):
        total = own[step, my_x, my_core].astype(jnp.float32)
        total = total + near[step, my_x].astype(jnp.float32)
        total = (total + far[step].astype(jnp.float32)).astype(jnp.bfloat16)
        if step == 0:
            home[1][0] = total
        else:
            home[0][step - 1] = total
            send(home_copy(*home, step))

    for step in order:
        if step % 2 == 0:
            mid_copy(step).wait_recv()
        send_home(glat, near_lat, far_lat, lat_home, step)
    remote(mid_key, far_key, mid_s.at[owners], mid_r.at[owners], head=across).wait_recv()
    for step in order:
        send_home(gkey, near_key, far_key, key_home, step)
    for home in (lat_home, key_home):
        for step in range(1, owners):
            home_copy(*home, step).wait_recv()
    for copy in sends:
        copy.wait_send()


def place_kernel(
    owners,
    home_ref,
    lat_ref,
    key_ref,
    qg_in,
    iqg_in,
    iwg_in,
    lat_out,
    key_out,
    qg_out,
    iqg_out,
    iwg_out,
    lat_buf,
    key_buf,
    small_sem,
    part_sem,
):
    copies = [
        pltpu.make_async_copy(src, dst, small_sem.at[number])
        for number, (src, dst) in enumerate(
            ((qg_in, qg_out), (iqg_in, iqg_out), (iwg_in, iwg_out))
        )
    ]
    for copy in copies:
        copy.start()
    lane = lax.broadcasted_iota(jnp.int32, (1, LANES), 1)
    told = home_ref[0:1, :]
    homes = [jnp.max(jnp.where(lane == step, told, 0)) for step in range(owners)]
    parts = part_sem.shape[1]
    span = lat_buf.shape[0] // parts
    for part in range(parts):
        here = pl.ds(part * span, span)
        lat_buf[here] = jnp.zeros((span, *lat_buf.shape[1:]), jnp.float32)
        key_buf[here] = jnp.zeros((span, *key_buf.shape[1:]), jnp.float32)
        for step in range(owners):
            at = homes[step]

            @pl.when((at >= part * span) & (at < (part + 1) * span))
            def _():
                lat_buf[at] = lat_buf[at] + lat_ref[step].astype(jnp.float32)
                key_buf[at] = key_buf[at] + key_ref[step].astype(jnp.float32)

        for kind, (buf, out) in enumerate(((lat_buf, lat_out), (key_buf, key_out))):
            copies.append(
                pltpu.make_async_copy(buf.at[here], out.at[here], part_sem.at[kind, part])
            )
            copies[-1].start()
    for copy in copies:
        copy.wait()


def shards(
    queries, out_grad, latents, index_keys, index_queries, index_weights, picked_blocks, key_reach
):
    owners = lax.axis_size("ctx")
    heads = lax.axis_size("head")
    row_count, local_heads, key_width = queries.shape
    latent_width = out_grad.shape[2]
    own_count, shard_rows = latents.shape[:2]
    index_width = index_keys.shape[2]
    context = key_reach.shape[0]
    block_rows = shard_rows * heads
    wide = -(-key_width // LANES) * LANES + index_width
    sizes = (row_count, local_heads, key_width, latent_width, shard_rows, context)
    low, full, whole = jnp.bfloat16, jnp.float32, jnp.int32
    vmem = pl.BlockSpec(memory_space=pltpu.VMEM)
    anywhere = pl.BlockSpec(memory_space=pl.ANY)
    sem = pltpu.SemaphoreType.DMA
    side = owners - 1
    query_grad, back_lat, back_key, iquery_grad, weight_grad, home = pl.pallas_call(
        functools.partial(exchange_kernel, owners, heads, sizes),
        out_shape=(
            pltpu.VMEM(queries.shape, low),
            pltpu.VMEM((owners, shard_rows, key_width), low),
            pltpu.VMEM((owners, shard_rows, index_width), low),
            pltpu.VMEM(index_queries.shape, low),
            pltpu.VMEM(index_weights.shape, full),
            pltpu.VMEM((8, LANES), whole),
        ),
        in_specs=[anywhere] * 8,
        out_specs=(vmem,) * 6,
        scratch_shapes=[
            pltpu.VMEM(index_queries.shape, low),
            pltpu.VMEM(index_weights.shape, full),
            pltpu.VMEM(picked_blocks.shape[::-1], whole),
            pltpu.VMEM(queries.shape, low),
            pltpu.VMEM(out_grad.shape, low),
            pltpu.VMEM(latents.shape, low),
            pltpu.VMEM(index_keys.shape, low),
            pltpu.VMEM((context // block_rows, block_rows), whole),
            pltpu.VMEM((8, LANES), whole),
            pltpu.VMEM((side, 8, LANES), whole),
            pltpu.VMEM((side, shard_rows, wide), low),
            pltpu.VMEM((owners, heads // 2, 2, shard_rows, wide), low),
            pltpu.VMEM((heads, 2, owners, row_count, block_rows), full),
            pltpu.VMEM((owners, heads // 2, 2, shard_rows, key_width), low),
            pltpu.VMEM((owners, heads // 2, 2, shard_rows, index_width), low),
            pltpu.VMEM((owners, heads // 2, shard_rows, key_width), low),
            pltpu.VMEM((owners, heads // 2, shard_rows, index_width), low),
            pltpu.VMEM((owners, shard_rows, key_width), low),
            pltpu.VMEM((owners, shard_rows, index_width), low),
            pltpu.VMEM((owners, shard_rows, key_width), low),
            pltpu.VMEM((owners, shard_rows, index_width), low),
            pltpu.VMEM((side, shard_rows, key_width), low),
            pltpu.VMEM((side, shard_rows, index_width), low),
            sem((8,)),
            sem((side,)),
            sem((side,)),
            sem((side,)),
            sem((side,)),
            sem((owners, 2)),
            sem((owners, 2)),
            sem((2, 3)),
            sem((2, 3)),
            sem((owners + 1,)),
            sem((owners + 1,)),
            sem((owners + 1,)),
            sem((owners + 1,)),
            sem((side,)),
            sem((side,)),
            sem((side,)),
            sem((side,)),
        ],
        compiler_params=pltpu.CompilerParams(
            collective_id=0, has_side_effects=True, vmem_limit_bytes=VMEM_BYTES
        ),
        name="exchange",
    )(
        queries,
        out_grad,
        latents,
        index_keys,
        index_queries,
        index_weights,
        picked_blocks.T,
        key_reach.reshape(context // block_rows, block_rows),
    )
    latent_grad, index_key_grad, query_grad, iquery_grad, weight_grad = pl.pallas_call(
        functools.partial(place_kernel, owners),
        out_shape=(
            jax.ShapeDtypeStruct((own_count, shard_rows, key_width), full),
            jax.ShapeDtypeStruct((own_count, shard_rows, index_width), full),
            jax.ShapeDtypeStruct(queries.shape, low),
            jax.ShapeDtypeStruct(index_queries.shape, low),
            jax.ShapeDtypeStruct(index_weights.shape, full),
        ),
        in_specs=[vmem] * 6,
        out_specs=(anywhere,) * 5,
        scratch_shapes=[
            pltpu.VMEM((own_count, shard_rows, key_width), full),
            pltpu.VMEM((own_count, shard_rows, index_width), full),
            sem((3,)),
            sem((2, 4)),
        ],
        compiler_params=pltpu.CompilerParams(vmem_limit_bytes=VMEM_BYTES),
        name="place",
    )(
        *(
            pltpu.with_memory_space_constraint(found, pltpu.VMEM)
            for found in (home, back_lat, back_key, query_grad, iquery_grad, weight_grad)
        )
    )
    return (query_grad, latent_grad, iquery_grad, weight_grad, index_key_grad)


def solution(mesh):
    placed = (
        P(("groups", "ctx"), "head", None),
        P(("groups", "ctx"), "head", None),
        P(None, ("groups", "ctx", "head"), None),
        P(None, ("groups", "ctx", "head"), None),
        P(("groups", "ctx"), "head", None),
        P(("groups", "ctx"), "head"),
        P(("groups", "ctx"), None),
        P("groups"),
    )
    return jax.shard_map(
        shards,
        mesh=mesh,
        in_specs=placed,
        out_specs=(
            P(("groups", "ctx"), "head", None),
            P(None, ("groups", "ctx", "head"), None),
            P(("groups", "ctx"), "head", None),
            P(("groups", "ctx"), "head"),
            P(None, ("groups", "ctx", "head"), None),
        ),
        check_vma=False,
    )
```

```python
import functools

import jax
import jax.numpy as jnp
from jax import lax
from jax.experimental import pallas as pl
from jax.experimental.pallas import tpu as pltpu
from jax.sharding import PartitionSpec as P

HEADS = 128
QK_DIM = 192
SCORE_FLOOR = -1e30
LANES = 128
MESH = pl.DeviceIdType.MESH
VMEM_BYTES = 56 * 1024 * 1024

NT = (((1,), (1,)), ((), ()))
TN = (((0,), (0,)), ((), ()))
NN = (((1,), (0,)), ((), ()))


def dot(a, b, dims):
    return lax.dot_general(a, b, dims, preferred_element_type=jnp.float32)


def exchange_kernel(
    owners,
    heads,
    sizes,
    q_hbm,
    g_hbm,
    lat_hbm,
    key_hbm,
    iq_hbm,
    iw_hbm,
    pick_hbm,
    reach_hbm,
    qg_ref,
    back_lat_ref,
    back_key_ref,
    iqg_ref,
    iwg_ref,
    home_ref,
    iq_ref,
    iw_ref,
    pick_ref,
    q_buf,
    g_buf,
    lat_buf,
    key_buf,
    reach_buf,
    want_buf,
    asked,
    row_send,
    rows,
    part,
    glat,
    gkey,
    near_lat,
    near_key,
    mid_lat,
    mid_key,
    far_lat,
    far_key,
    hlat,
    hkey,
    local_sem,
    ask_s,
    ask_r,
    row_s,
    row_r,
    fwd_s,
    fwd_r,
    part_s,
    part_r,
    near_s,
    near_r,
    mid_s,
    mid_r,
    hlat_s,
    hlat_r,
    hkey_s,
    hkey_r,
):
    row_count, local_heads, key_width, latent_width, shard_rows, context = sizes
    key_at = -(-key_width // LANES) * LANES
    block_rows = shard_rows * heads
    shift = owners.bit_length() - 1
    me_c = lax.axis_index("ctx")
    me_h = lax.axis_index("head")
    my_x, my_core = me_h // 2, lax.rem(me_h, 2)
    beside = me_h + 1 - 2 * my_core
    across = lax.rem(me_h + 2, heads)
    opposite = heads - 1 - me_h
    others = (beside, across, opposite)

    def ctx_at(step):
        found = me_c
        for bit in range(shift):
            if step >> bit & 1:
                found = found + (1 << bit) * (1 - 2 * lax.rem(me_c // (1 << bit), 2))
        return found

    def remote(src, dst, send_sem, recv_sem, **where):
        return pltpu.make_async_remote_copy(
            src_ref=src,
            dst_ref=dst,
            send_sem=send_sem,
            recv_sem=recv_sem,
            device_id=where,
            device_id_type=MESH,
        )

    sends = []

    def send(copy):
        copy.start()
        sends.append(copy)

    loads = [
        pltpu.make_async_copy(src, dst, local_sem.at[number])
        for number, (src, dst) in enumerate(
            (
                (lat_hbm, lat_buf),
                (key_hbm, key_buf),
                (reach_hbm, reach_buf),
                (q_hbm, q_buf),
                (g_hbm, g_buf),
                (iq_hbm, iq_ref),
                (iw_hbm, iw_ref),
                (pick_hbm, pick_ref),
            )
        )
    ]
    barrier = pltpu.get_barrier_semaphore()
    for step in range(1, owners):
        pl.semaphore_signal(
            barrier, inc=1, device_id={"ctx": ctx_at(step)}, device_id_type=MESH
        )
    for other in others:
        pl.semaphore_signal(barrier, inc=1, device_id={"head": other}, device_id_type=MESH)
    for load in (loads[7], *loads[:7]):
        load.start()
    loads[7].wait()

    lane = lax.broadcasted_iota(jnp.int32, (row_count, LANES), 1)
    diagonal = lax.broadcasted_iota(
        jnp.int32, (row_count, row_count), 0
    ) == lax.broadcasted_iota(jnp.int32, (row_count, row_count), 1)
    by_row = jnp.full((row_count, LANES), -1, jnp.int32)
    for number in range(pick_ref.shape[0]):
        line = jnp.broadcast_to(pick_ref[number : number + 1, :], (row_count, row_count))
        column = jnp.max(jnp.where(diagonal, line, -1), axis=1, keepdims=True)
        column = jnp.broadcast_to(column, (row_count, LANES))
        match = (column >= 0) & ((column & (owners - 1)) == lane)
        by_row = jnp.where(match, column >> shift, by_row)
    wanted = jnp.max(by_row, axis=0, keepdims=True)
    want_buf[...] = jnp.broadcast_to(wanted, want_buf.shape)
    pl.semaphore_wait(barrier, owners + heads - 2)

    asks = []
    for step in range(1, owners):
        asks.append(
            remote(
                want_buf,
                asked.at[step - 1],
                ask_s.at[step - 1],
                ask_r.at[step - 1],
                ctx=ctx_at(step),
            )
        )
        send(asks[-1])

    def hand_across(step, x):
        slot = rows.at[step, x, my_core]
        return remote(slot, slot, fwd_s.at[step, 0], fwd_r.at[step, 0], head=across)

    def hand_beside(step, core):
        slot = rows.at[step, :, core]
        return remote(slot, slot, fwd_s.at[step, 1], fwd_r.at[step, 1], head=beside)

    loads[0].wait()
    loads[1].wait()
    first_lane = lax.broadcasted_iota(jnp.int32, (1, LANES), 1)
    own_round = jnp.max(jnp.where(first_lane == me_c, wanted, -1))
    at = jnp.maximum(own_round, 0)
    rows[0, my_x, my_core, :, :key_width] = lat_buf[at]
    rows[0, my_x, my_core, :, key_at:] = key_buf[at]
    homes = [own_round]
    for step in range(1, owners):
        asks[step - 1].wait_recv()
        told = jnp.max(jnp.where(first_lane == me_c, asked[step - 1, 0:1, :], -1))
        homes.append(told)
        at = jnp.maximum(told, 0)
        row_send[step - 1, :, :key_width] = lat_buf[at]
        row_send[step - 1, :, key_at:] = key_buf[at]
        send(
            remote(
                row_send.at[step - 1],
                rows.at[step, my_x, my_core],
                row_s.at[step - 1],
                row_r.at[step - 1],
                ctx=ctx_at(step),
            )
        )
    send(hand_across(0, my_x))
    home_lane = lax.broadcasted_iota(jnp.int32, home_ref.shape, 1)
    home_all = jnp.full(home_ref.shape, -1, jnp.int32)
    for step in range(owners):
        home_all = jnp.where(home_lane == step, homes[step], home_all)
    home_ref[...] = home_all

    loads[2].wait()
    first_pos = context - row_count * owners + me_c * row_count
    places = first_pos + lax.broadcasted_iota(jnp.int32, (row_count, block_rows), 0)
    offsets = lax.broadcasted_iota(jnp.int32, (row_count, block_rows), 1)
    seen = []
    for step in range(owners):
        owner = ctx_at(step)
        block = (
            jnp.maximum(jnp.max(jnp.where(first_lane == owner, wanted, -1)), 0) * owners + owner
        )
        ends = jnp.broadcast_to(reach_buf[pl.ds(block, 1), :], places.shape)
        used = jnp.max(jnp.where(lane == owner, by_row, -1), axis=1, keepdims=True)
        used = jnp.broadcast_to(used, places.shape) >= 0
        ok = used & (block * block_rows + offsets <= places) & (places < ends)
        seen.append(jnp.where(ok, 1.0, 0.0))

    for load in loads[3:7]:
        load.wait()
    stack = row_count * local_heads
    queries = q_buf[...].reshape(stack, key_width)
    grads = g_buf[...].reshape(stack, latent_width)
    index_heads, index_width = iq_ref.shape[1], iq_ref.shape[2]
    index_stack = row_count * index_heads
    iqueries = iq_ref[...].reshape(index_stack, index_width)
    eye = jnp.where(
        lax.broadcasted_iota(jnp.int32, (index_heads, index_heads), 0)
        == lax.broadcasted_iota(jnp.int32, (index_heads, index_heads), 1),
        1.0,
        0.0,
    )
    weights = jnp.sum(iw_ref[...][:, None, :] * eye[None], axis=2, keepdims=True)
    score_scale = QK_DIM ** (-0.5)
    index_scores, scores, pulls = [], [], []

    def keys_of(step):
        return rows[step, :, :, :, :key_width].reshape(block_rows, key_width)

    def ikeys_of(step):
        return rows[step, :, :, :, key_at:].reshape(block_rows, index_width)

    def multiply(step):
        found = dot(iqueries, ikeys_of(step), NT).reshape(row_count, index_heads, block_rows)
        index_scores.append(found)
        part[me_h, 1, step] = jnp.sum(weights * jnp.maximum(found, 0.0), axis=1)
        keys = keys_of(step)
        found = dot(queries, keys, NT).reshape(row_count, local_heads, block_rows) * score_scale
        scores.append(jnp.where(seen[step][:, None, :] > 0.5, found, SCORE_FLOOR))
        found = dot(grads, keys[:, :latent_width], NT)
        pulls.append(found.reshape(row_count, local_heads, block_rows))

    for turn in range(owners + 2):
        if turn < owners and turn > 0:
            remote(
                row_send.at[0],
                rows.at[turn, my_x, my_core],
                row_s.at[turn - 1],
                row_r.at[turn - 1],
                ctx=ctx_at(turn),
            ).wait_recv()
            send(hand_across(turn, my_x))
        if 1 <= turn <= owners:
            hand_across(turn - 1, 1 - my_x).wait_recv()
            send(hand_beside(turn - 1, my_core))
        if turn >= 2:
            hand_beside(turn - 2, 1 - my_core).wait_recv()
            multiply(turn - 2)

    def share(kind):
        for number, other in enumerate(others):
            slot = part.at[me_h, kind]
            send(remote(slot, slot, part_s.at[kind, number], part_r.at[kind, number], head=other))

    def softmax(chunks):
        top = functools.reduce(jnp.maximum, chunks)
        top = jnp.max(top, axis=-1, keepdims=True)
        raised = [jnp.exp(chunk - top) for chunk in chunks]
        total = jnp.sum(functools.reduce(jnp.add, raised), axis=-1, keepdims=True)
        inverse = 1.0 / total
        return [chunk * inverse for chunk in raised]

    share(1)
    attention = softmax(scores)
    for step in range(owners):
        part[me_h, 0, step] = jnp.sum(attention[step], axis=1)
    share(0)
    inner = functools.reduce(jnp.add, [a * p for a, p in zip(attention, pulls)])
    inner = jnp.sum(inner, axis=-1, keepdims=True)
    order = [first + more for first in range(owners - 2, -1, -2) for more in range(2)]

    def near_copy(first):
        two = pl.ds(first, 2)
        return remote(
            glat.at[two, :, 1 - my_core],
            near_lat.at[two],
            near_s.at[first],
            near_r.at[first],
            head=beside,
        )

    def mid_copy(first):
        two = pl.ds(first, 2)
        return remote(
            mid_lat.at[two], far_lat.at[two], mid_s.at[first], mid_r.at[first], head=across
        )

    score_grads = [None] * owners
    shape = (heads // 2, 2, shard_rows)
    for step in order:
        found = score_scale * attention[step] * (pulls[step] - inner)
        found = found.astype(jnp.bfloat16).reshape(stack, block_rows)
        score_grads[step] = found
        low = attention[step].astype(jnp.bfloat16).reshape(stack, block_rows)
        key_grad = dot(found, queries, TN)
        value_grad = dot(low, grads, TN)
        front = (key_grad[:, :latent_width] + value_grad).astype(jnp.bfloat16)
        glat[step, :, :, :, :latent_width] = front.reshape(*shape, latent_width)
        rest = key_grad[:, latent_width:].astype(jnp.bfloat16)
        glat[step, :, :, :, latent_width:] = rest.reshape(*shape, key_width - latent_width)
        if step % 2:
            send(near_copy(step - 1))

    found = jnp.zeros((stack, key_width), jnp.float32)
    for step in range(owners):
        found = found + dot(score_grads[step], keys_of(step), NN)
    qg_ref[...] = found.astype(jnp.bfloat16).reshape(row_count, local_heads, key_width)

    for step in order:
        if step % 2 == 0:
            near_copy(step).wait_recv()
        total = glat[step, 1 - my_x, my_core].astype(jnp.float32)
        total = total + near_lat[step, 1 - my_x].astype(jnp.float32)
        mid_lat[step] = total.astype(jnp.bfloat16)
        if step % 2:
            send(mid_copy(step - 1))

    for kind in range(2):
        for number, other in enumerate(others):
            slot = part.at[other, kind]
            remote(
                slot, slot, part_s.at[kind, number], part_r.at[kind, number], head=other
            ).wait_recv()

    def total_of(kind, step):
        found = part[0, kind, step]
        for head in range(1, heads):
            found = found + part[head, kind, step]
        return found

    logits = [
        jnp.where(seen[step] > 0.5, total_of(1, step), SCORE_FLOOR) for step in range(owners)
    ]
    probs = softmax(logits)
    logit_grads = [probs[step] - total_of(0, step) * (1.0 / HEADS) for step in range(owners)]

    spreads = []
    for step in range(owners):
        found = jnp.where(
            index_scores[step] > 0.0, logit_grads[step][:, None, :] * weights, 0.0
        )
        found = found.astype(jnp.bfloat16).reshape(index_stack, block_rows)
        spreads.append(found)
        found = dot(found, iqueries, TN).astype(jnp.bfloat16)
        gkey[step] = found.reshape(*shape, index_width)
    send(
        remote(
            gkey.at[:, :, 1 - my_core],
            near_key,
            near_s.at[owners],
            near_r.at[owners],
            head=beside,
        )
    )
    remote(
        gkey.at[:, :, 0], near_key, near_s.at[owners], near_r.at[owners], head=beside
    ).wait_recv()
    for step in range(owners):
        total = gkey[step, 1 - my_x, my_core].astype(jnp.float32)
        total = total + near_key[step, 1 - my_x].astype(jnp.float32)
        mid_key[step] = total.astype(jnp.bfloat16)
    send(remote(mid_key, far_key, mid_s.at[owners], mid_r.at[owners], head=across))

    def home_copy(out, back_ref, out_s, out_r, step):
        return remote(
            out.at[step - 1],
            back_ref.at[step],
            out_s.at[step - 1],
            out_r.at[step - 1],
            ctx=ctx_at(step),
        )

    lat_home = (hlat, back_lat_ref, hlat_s, hlat_r)
    key_home = (hkey, back_key_ref, hkey_s, hkey_r)

    def send_home(own, near, far, home, step):
        total = own[step, my_x, my_core].astype(jnp.float32)
        total = total + near[step, my_x].astype(jnp.float32)
        total = (total + far[step].astype(jnp.float32)).astype(jnp.bfloat16)
        if step == 0:
            home[1][0] = total
        else:
            home[0][step - 1] = total
            send(home_copy(*home, step))

    mid_copy(order[0]).wait_recv()
    for step in order[:2]:
        send_home(glat, near_lat, far_lat, lat_home, step)

    found = jnp.zeros((index_stack, index_width), jnp.float32)
    weight_grad = jnp.zeros((row_count, index_heads, block_rows), jnp.float32)
    for step in range(owners):
        found = found + dot(spreads[step], ikeys_of(step), NN)
        weight_grad = weight_grad + logit_grads[step][:, None, :] * jnp.maximum(
            index_scores[step], 0.0
        )
    iqg_ref[...] = found.astype(jnp.bfloat16).reshape(row_count, index_heads, index_width)
    weight_grad = jnp.sum(weight_grad, axis=-1, keepdims=True)
    iwg_ref[...] = jnp.sum(weight_grad * eye[None], axis=1)

    for step in order[2:]:
        if step % 2 == 0:
            mid_copy(step).wait_recv()
        send_home(glat, near_lat, far_lat, lat_home, step)
    remote(mid_key, far_key, mid_s.at[owners], mid_r.at[owners], head=across).wait_recv()
    for step in order:
        send_home(gkey, near_key, far_key, key_home, step)
    for home in (lat_home, key_home):
        for step in range(1, owners):
            home_copy(*home, step).wait_recv()
    for copy in sends:
        copy.wait_send()


def place_kernel(
    owners,
    home_ref,
    lat_ref,
    key_ref,
    qg_in,
    iqg_in,
    iwg_in,
    lat_out,
    key_out,
    qg_out,
    iqg_out,
    iwg_out,
    lat_buf,
    key_buf,
    small_sem,
    part_sem,
):
    copies = [
        pltpu.make_async_copy(src, dst, small_sem.at[number])
        for number, (src, dst) in enumerate(
            ((qg_in, qg_out), (iqg_in, iqg_out), (iwg_in, iwg_out))
        )
    ]
    for copy in copies:
        copy.start()
    lane = lax.broadcasted_iota(jnp.int32, (1, LANES), 1)
    told = home_ref[0:1, :]
    homes = [jnp.max(jnp.where(lane == step, told, 0)) for step in range(owners)]
    parts = part_sem.shape[1]
    span = lat_buf.shape[0] // parts
    for part in range(parts):
        here = pl.ds(part * span, span)
        lat_buf[here] = jnp.zeros((span, *lat_buf.shape[1:]), jnp.float32)
        key_buf[here] = jnp.zeros((span, *key_buf.shape[1:]), jnp.float32)
        for step in range(owners):
            at = homes[step]

            @pl.when((at >= part * span) & (at < (part + 1) * span))
            def _():
                lat_buf[at] = lat_buf[at] + lat_ref[step].astype(jnp.float32)
                key_buf[at] = key_buf[at] + key_ref[step].astype(jnp.float32)

        for kind, (buf, out) in enumerate(((lat_buf, lat_out), (key_buf, key_out))):
            copies.append(
                pltpu.make_async_copy(buf.at[here], out.at[here], part_sem.at[kind, part])
            )
            copies[-1].start()
    for copy in copies:
        copy.wait()


def shards(
    queries, out_grad, latents, index_keys, index_queries, index_weights, picked_blocks, key_reach
):
    owners = lax.axis_size("ctx")
    heads = lax.axis_size("head")
    row_count, local_heads, key_width = queries.shape
    latent_width = out_grad.shape[2]
    own_count, shard_rows = latents.shape[:2]
    index_width = index_keys.shape[2]
    context = key_reach.shape[0]
    block_rows = shard_rows * heads
    wide = -(-key_width // LANES) * LANES + index_width
    sizes = (row_count, local_heads, key_width, latent_width, shard_rows, context)
    low, full, whole = jnp.bfloat16, jnp.float32, jnp.int32
    vmem = pl.BlockSpec(memory_space=pltpu.VMEM)
    anywhere = pl.BlockSpec(memory_space=pl.ANY)
    sem = pltpu.SemaphoreType.DMA
    side = owners - 1
    query_grad, back_lat, back_key, iquery_grad, weight_grad, home = pl.pallas_call(
        functools.partial(exchange_kernel, owners, heads, sizes),
        out_shape=(
            pltpu.VMEM(queries.shape, low),
            pltpu.VMEM((owners, shard_rows, key_width), low),
            pltpu.VMEM((owners, shard_rows, index_width), low),
            pltpu.VMEM(index_queries.shape, low),
            pltpu.VMEM(index_weights.shape, full),
            pltpu.VMEM((8, LANES), whole),
        ),
        in_specs=[anywhere] * 8,
        out_specs=(vmem,) * 6,
        scratch_shapes=[
            pltpu.VMEM(index_queries.shape, low),
            pltpu.VMEM(index_weights.shape, full),
            pltpu.VMEM(picked_blocks.shape[::-1], whole),
            pltpu.VMEM(queries.shape, low),
            pltpu.VMEM(out_grad.shape, low),
            pltpu.VMEM(latents.shape, low),
            pltpu.VMEM(index_keys.shape, low),
            pltpu.VMEM((context // block_rows, block_rows), whole),
            pltpu.VMEM((8, LANES), whole),
            pltpu.VMEM((side, 8, LANES), whole),
            pltpu.VMEM((side, shard_rows, wide), low),
            pltpu.VMEM((owners, heads // 2, 2, shard_rows, wide), low),
            pltpu.VMEM((heads, 2, owners, row_count, block_rows), full),
            pltpu.VMEM((owners, heads // 2, 2, shard_rows, key_width), low),
            pltpu.VMEM((owners, heads // 2, 2, shard_rows, index_width), low),
            pltpu.VMEM((owners, heads // 2, shard_rows, key_width), low),
            pltpu.VMEM((owners, heads // 2, shard_rows, index_width), low),
            pltpu.VMEM((owners, shard_rows, key_width), low),
            pltpu.VMEM((owners, shard_rows, index_width), low),
            pltpu.VMEM((owners, shard_rows, key_width), low),
            pltpu.VMEM((owners, shard_rows, index_width), low),
            pltpu.VMEM((side, shard_rows, key_width), low),
            pltpu.VMEM((side, shard_rows, index_width), low),
            sem((8,)),
            sem((side,)),
            sem((side,)),
            sem((side,)),
            sem((side,)),
            sem((owners, 2)),
            sem((owners, 2)),
            sem((2, 3)),
            sem((2, 3)),
            sem((owners + 1,)),
            sem((owners + 1,)),
            sem((owners + 1,)),
            sem((owners + 1,)),
            sem((side,)),
            sem((side,)),
            sem((side,)),
            sem((side,)),
        ],
        compiler_params=pltpu.CompilerParams(
            collective_id=0, has_side_effects=True, vmem_limit_bytes=VMEM_BYTES
        ),
        name="exchange",
    )(
        queries,
        out_grad,
        latents,
        index_keys,
        index_queries,
        index_weights,
        picked_blocks.T,
        key_reach.reshape(context // block_rows, block_rows),
    )
    latent_grad, index_key_grad, query_grad, iquery_grad, weight_grad = pl.pallas_call(
        functools.partial(place_kernel, owners),
        out_shape=(
            jax.ShapeDtypeStruct((own_count, shard_rows, key_width), full),
            jax.ShapeDtypeStruct((own_count, shard_rows, index_width), full),
            jax.ShapeDtypeStruct(queries.shape, low),
            jax.ShapeDtypeStruct(index_queries.shape, low),
            jax.ShapeDtypeStruct(index_weights.shape, full),
        ),
        in_specs=[vmem] * 6,
        out_specs=(anywhere,) * 5,
        scratch_shapes=[
            pltpu.VMEM((own_count, shard_rows, key_width), full),
            pltpu.VMEM((own_count, shard_rows, index_width), full),
            sem((3,)),
            sem((2, 4)),
        ],
        compiler_params=pltpu.CompilerParams(vmem_limit_bytes=VMEM_BYTES),
        name="place",
    )(
        *(
            pltpu.with_memory_space_constraint(found, pltpu.VMEM)
            for found in (home, back_lat, back_key, query_grad, iquery_grad, weight_grad)
        )
    )
    return (query_grad, latent_grad, iquery_grad, weight_grad, index_key_grad)


def solution(mesh):
    placed = (
        P(("groups", "ctx"), "head", None),
        P(("groups", "ctx"), "head", None),
        P(None, ("groups", "ctx", "head"), None),
        P(None, ("groups", "ctx", "head"), None),
        P(("groups", "ctx"), "head", None),
        P(("groups", "ctx"), "head"),
        P(("groups", "ctx"), None),
        P("groups"),
    )
    return jax.shard_map(
        shards,
        mesh=mesh,
        in_specs=placed,
        out_specs=(
            P(("groups", "ctx"), "head", None),
            P(None, ("groups", "ctx", "head"), None),
            P(("groups", "ctx"), "head", None),
            P(("groups", "ctx"), "head"),
            P(None, ("groups", "ctx", "head"), None),
        ),
        check_vma=False,
    )
```
